32 devices in a mesh: sub: 2 (over x), gate: 16 (over z, y, core).
Axes of the slice: x: 2, y: 2, z: 4, core: 2. Of those that a mesh axis runs over, the one named last changes fastest.
Arguments:
- raw_echo: bfloat16 [2, 256, 16384], P(None, ('sub', 'gate')), may hold values from -6 to 6
- delays: int32 [256], P(('sub', 'gate')), may hold values from 0 to 64
Outputs:
- image: bfloat16 [2, 512, 16384], P(None, 'sub', 'gate')
The draws below stay inside these ranges and needn't reach their ends.
All inputs are finite; a program needn't handle non-finite values.
Results may differ from the reference program's by a relative error of at most 0.009.
Values may be sent and summed in bfloat16 or wider, within the bound.
No kernel may reach another device: no remote copies, remote signals or barrier semaphores. Data moves between devices by JAX's collectives and lax.ppermute only.
A program may use at most 64 MiB of HBM per device.

```python
import math
import jax
import jax.numpy as jnp
from jax import lax

RADIX = 128
SAMPLES = 16384
ANGLES = 256
DELAY_MAX = 64
SUB_PULSES = 128
PULSES = 256
LEVELS = 1
N_SUB = 2


def with_ends(values, rng, smallest, largest):
    dims = values.shape
    spot = [jax.random.randint(jax.random.fold_in(rng, axis), (), 0, dims[axis]) for axis in range(len(dims))]
    values = values.at[tuple(spot)].set(smallest)
    longest = dims.index(max(dims))
    spot[longest] = (spot[longest] + 1) % dims[longest]
    return values.at[tuple(spot)].set(largest)


def block_scale(own_key, dims, shards, least, high):
    gain = 1.0
    for position, parts in shards:
        draws = jax.random.uniform(jax.random.fold_in(jax.random.fold_in(own_key, 6), position), (parts,), jnp.float32, least / len(shards), high / len(shards))
        gain = gain * jnp.repeat(jnp.exp(draws), dims[position] // parts).reshape((-1,) + (1,) * (len(dims) - 1 - position))
    return gain


def scatter_about(stream_key, shape, width, reach, shards=(), kind=jnp.bfloat16):
    drawn = width * jax.random.normal(stream_key, shape, jnp.float32)
    if shards:
        drawn = drawn * block_scale(stream_key, shape, shards, -0.22, 0.18)
    return jnp.clip(drawn, -reach, reach).astype(kind)


def setup_inputs(seed: int = 0) -> dict:
    seeds = jax.random.split(jax.random.key(seed), 3)
    return {
        "raw_echo": scatter_about(seeds[0], (2, PULSES, SAMPLES), 1.0, 6.0, ((1, 32),)),
        "delays": with_ends(jax.random.randint(seeds[1], (PULSES,), 0, DELAY_MAX + 1), jax.random.fold_in(seeds[1], 1), 0, DELAY_MAX).astype(jnp.int32),
    }


TWO_PI = 2.0 * math.pi

def complex_blocks(real_part, imag_part):
    upper = jnp.stack([real_part, -imag_part], axis=1)
    lower = jnp.stack([imag_part, real_part], axis=1)
    return jnp.stack([upper, lower], axis=0).astype(jnp.bfloat16)

def dft_blocks(order):
    counter = jnp.arange(order, dtype=jnp.int32)
    product = counter[:, None] * counter[None, :] % order
    phases = -TWO_PI / order * product.astype(jnp.float32)
    factor = 1.0 / math.sqrt(order)
    return complex_blocks(jnp.cos(phases) * factor, jnp.sin(phases) * factor)

def steer_blocks(beam_count, pulse_count):
    beam_index = jnp.arange(beam_count, dtype=jnp.int32)
    pulse_index = jnp.arange(pulse_count, dtype=jnp.int32)
    modulus = 16 * beam_count
    product = (2 * beam_index[:, None] - beam_count + 1) * (2 * pulse_index[None, :] - pulse_count + 1) % modulus
    phases = -TWO_PI / modulus * product.astype(jnp.float32)
    factor = 1.0 / math.sqrt(pulse_count)
    return complex_blocks(jnp.cos(phases) * factor, jnp.sin(phases) * factor)

def interp_table(beam_count):
    half_count = beam_count // 2
    targets = jnp.arange(beam_count, dtype=jnp.float32)
    sources = jnp.arange(half_count, dtype=jnp.float32)
    distance = targets[:, None] * 0.5 - 0.25 - sources[None, :]
    taper = jnp.where(jnp.abs(distance) < 4.0, 0.5 + 0.5 * jnp.cos(math.pi * distance / 4.0), 0.0)
    return (jnp.sinc(distance) * taper).astype(jnp.bfloat16)

def rotation(center, numerator, depth, gate_pos):
    modulus = ANGLES * 2 ** (depth + 3)
    turns = jnp.mod(center * numerator, modulus).astype(jnp.float32) / modulus
    center_sq = (center * center).astype(jnp.float32)
    near_term = center_sq / (16.0 * (SAMPLES + gate_pos))
    phases = -TWO_PI * turns[:, None] - TWO_PI / (4 * ANGLES) * near_term[None, :]
    factor = 1.0 / math.sqrt(2.0)
    return (jnp.cos(phases) * factor, jnp.sin(phases) * factor)

def range_compress(raw_block, delay_block):
    pulse_count = raw_block.shape[1]
    dft_table = dft_blocks(RADIX).astype(jnp.float32)
    samples_grid = raw_block.reshape(2, pulse_count, RADIX, RADIX).astype(jnp.float32)
    section_one = jnp.einsum('akcn,cpnm->apkm', dft_table, samples_grid)
    counter = jnp.arange(RADIX, dtype=jnp.int32)
    phases = -TWO_PI / SAMPLES * (counter[:, None] * counter[None, :]).astype(jnp.float32)
    cosine = jnp.cos(phases)
    sine_part = jnp.sin(phases)
    twisted = jnp.stack([section_one[0] * cosine - section_one[1] * sine_part, section_one[0] * sine_part + section_one[1] * cosine]).astype(jnp.bfloat16)
    spectrum = jnp.einsum('akcn,cpjn->apkj', dft_table, twisted.astype(jnp.float32))
    spectrum = spectrum.reshape(2, pulse_count, SAMPLES)
    padded = jnp.pad(spectrum, ((0, 0), (0, 0), (0, DELAY_MAX)))

    def shift_row(pulse_row, start):
        return lax.dynamic_slice_in_dim(pulse_row, start, SAMPLES, axis=1)
    shifted = jax.vmap(shift_row, in_axes=(1, 0), out_axes=1)(padded, delay_block)
    return shifted.astype(jnp.bfloat16)

def merge_level(images, depth, gate_pos):
    pairs = images.shape[0] // 2
    half_count = ANGLES // 2
    sectors = 2 ** depth
    columns = images.shape[-1]
    child = images.reshape(pairs, 2, 2, sectors, half_count, columns).astype(jnp.float32)
    moved = jnp.einsum('jh,bkcqhg->bkcqjg', interp_table(ANGLES).astype(jnp.float32), child)
    row_index = jnp.arange(sectors * ANGLES, dtype=jnp.int32)
    numerator = 2 * row_index + 1 - ANGLES * sectors
    offset = SUB_PULSES * 2 ** (depth - 1) // 2
    total_real = jnp.zeros((pairs, sectors, ANGLES, columns), jnp.float32)
    total_imag = jnp.zeros((pairs, sectors, ANGLES, columns), jnp.float32)
    for member in range(2):
        center = jnp.asarray((2 * member - 1) * offset, dtype=jnp.int32)
        cosine, sine_part = rotation(center, numerator, depth, gate_pos)
        cosine = cosine.reshape(sectors, ANGLES, columns)
        sine_part = sine_part.reshape(sectors, ANGLES, columns)
        part_real = moved[:, member, 0]
        part_imag = moved[:, member, 1]
        total_real = total_real + cosine * part_real - sine_part * part_imag
        total_imag = total_imag + sine_part * part_real + cosine * part_imag
    merged = jnp.stack([total_real, total_imag], axis=1)
    return merged.reshape(pairs, 2, sectors * ANGLES, columns).astype(jnp.bfloat16)

def reverse_blocks(values, depth_count):
    columns = values.shape[-1]
    digits = values.reshape((2,) + (2,) * depth_count + (ANGLES, columns))
    axes_order = (0,) + tuple(range(depth_count, 0, -1)) + (depth_count + 1, depth_count + 2)
    return jnp.transpose(digits, axes_order).reshape(2, 2 ** depth_count, ANGLES, columns)

def reference(raw_echo, delays):
    steering = steer_blocks(ANGLES, SUB_PULSES).astype(jnp.float32)

    def one_sub(sub_number):
        raw_block = lax.dynamic_slice_in_dim(raw_echo, sub_number * SUB_PULSES, SUB_PULSES, axis=1)
        delay_block = lax.dynamic_slice_in_dim(delays, sub_number * SUB_PULSES, SUB_PULSES, axis=0)
        compressed = range_compress(raw_block, delay_block)
        return jnp.einsum('akcm,cmg->akg', steering, compressed.astype(jnp.float32)).astype(jnp.bfloat16)
    level_zero = lax.map(one_sub, jnp.arange(N_SUB, dtype=jnp.int32))
    block_count = 8
    block_width = SAMPLES // block_count
    gate_blocks = level_zero.reshape(N_SUB, 2, ANGLES, block_count, block_width).transpose(3, 0, 1, 2, 4)
    starts = jnp.arange(block_count, dtype=jnp.int32) * block_width

    def one_block(inputs):
        images, start = inputs
        gate_pos = (start + jnp.arange(block_width, dtype=jnp.int32)).astype(jnp.float32)
        for depth in range(1, LEVELS + 1):
            images = merge_level(images, depth, gate_pos)
        return images[0]
    merged = lax.map(one_block, (gate_blocks, starts))
    whole_image = merged.transpose(1, 2, 0, 3).reshape(2, ANGLES * N_SUB, SAMPLES)
    return reverse_blocks(whole_image, LEVELS).reshape(2, ANGLES * N_SUB, SAMPLES)
```

```python
import math

import jax
import jax.numpy as jnp
import numpy as np
from jax import lax
from jax.experimental import pallas as pl
from jax.experimental.pallas import tpu as pltpu
from jax.sharding import PartitionSpec as P

RADIX = 128
SAMPLES = 16384
ANGLES = 256
DELAY_MAX = 64
LANES = 128
ROWS = RADIX + DELAY_MAX


TWO_PI = 2.0 * math.pi


def to_bf16(values):
    return np.asarray(values, np.float32).astype(jnp.bfloat16)


def rounded(values):
    return to_bf16(values).astype(np.float64)


def real_form(table):
    upper = np.concatenate([table.real, -table.imag], axis=1)
    lower = np.concatenate([table.imag, table.real], axis=1)
    return np.concatenate([upper, lower], axis=0)


def unit(phases):
    return np.cos(phases) + 1j * np.sin(phases)


def dft_table():
    counter = np.arange(RADIX)
    table = unit(-TWO_PI / RADIX * (counter[:, None] * counter[None, :] % RADIX)) / math.sqrt(RADIX)
    return rounded(table.real) + 1j * rounded(table.imag)


def twiddles():
    phases = -TWO_PI / SAMPLES * (np.arange(ROWS)[:, None] * np.arange(RADIX)[None, :])
    return np.stack([np.cos(phases), np.sin(phases)]).astype(np.float32)


def near_phases(depth_count, sub_pulses):
    centers = [sub_pulses * 2 ** (depth - 1) // 2 for depth in range(1, depth_count + 1)]
    center_sq = float(sum(center * center for center in centers))
    phases = -TWO_PI / (4 * ANGLES) * center_sq / (16.0 * (SAMPLES + np.arange(SAMPLES)))
    return np.stack([np.cos(phases), np.sin(phases)]).astype(np.float32).reshape(2, RADIX, RADIX)


def steer_table(sub_pulses):
    modulus = 16 * ANGLES
    beams = 2 * np.arange(ANGLES) - ANGLES + 1
    pulses = 2 * np.arange(sub_pulses) - sub_pulses + 1
    table = unit(-TWO_PI / modulus * (beams[:, None] * pulses[None, :] % modulus)) / math.sqrt(sub_pulses)
    return rounded(table.real) + 1j * rounded(table.imag)


def interp_table():
    distance = np.arange(ANGLES)[:, None] * 0.5 - 0.25 - np.arange(ANGLES // 2)[None, :]
    taper = np.where(np.abs(distance) < 4.0, 0.5 + 0.5 * np.cos(math.pi * distance / 4.0), 0.0)
    return rounded(np.sinc(distance) * taper)


def merge_table(depth, sector, center):
    modulus = ANGLES * 2 ** (depth + 3)
    row_index = sector * ANGLES + np.arange(ANGLES)
    numerator = 2 * row_index + 1 - ANGLES * 2**depth
    turns = (center * numerator) % modulus / modulus
    return unit(-TWO_PI * turns)[:, None] * interp_table() / math.sqrt(2.0)


def by_source(table, pulse_count):
    rows = table.shape[0]
    return table.reshape(rows, 2, -1, pulse_count).transpose(0, 2, 1, 3).reshape(rows, -1)


def image_tables(sub_pulses, pulse_count):
    half = ANGLES // 2
    steer = steer_table(sub_pulses)
    tables = []
    for sub in range(2):
        beams = steer[sub * half : (sub + 1) * half]
        own = (2 * sub - 1) * (sub_pulses // 2)
        parts = [real_form(merge_table(1, sub, center) @ beams) for center in (own, -own)]
        tables.append(np.concatenate([by_source(part, pulse_count) for part in parts], axis=1))
    return to_bf16(np.stack(tables))


def compress_kernel(
    delays, raw, first, second, twiddle, near, out, lines, grid_in, section, twisted, turned
):
    pulse_count = raw.shape[1]
    blocks, _, width = out.shape
    span = RADIX * pulse_count
    for part in range(2):
        for step in range(RADIX):
            lines[pl.ds(part * span + step * pulse_count, pulse_count), :] = raw[
                part, :, pl.ds(step * LANES, LANES)
            ].astype(jnp.float32)
    for part in range(2):
        for pulse in range(pulse_count):
            grid_in[pl.ds(part * RADIX, RADIX), pl.ds(pulse * LANES, LANES)] = lines[
                pl.ds(part * span + pulse, RADIX, stride=pulse_count), :
            ].astype(jnp.bfloat16)
    for pulse in range(pulse_count):
        columns = pl.ds(pulse * LANES, LANES)
        sums = jnp.dot(first[...], grid_in[:, columns], preferred_element_type=jnp.float32)
        for part in range(2):
            own = sums[part * RADIX : (part + 1) * RADIX]
            section[pulse, part, pl.ds(0, RADIX), :] = own
            section[pulse, part, pl.ds(RADIX, DELAY_MAX), :] = own[:DELAY_MAX]
    for pulse in range(pulse_count):
        window = pl.ds(delays[pulse], RADIX)
        real_part = section[pulse, 0, window, :]
        imag_part = section[pulse, 1, window, :]
        cosine = twiddle[0, window, :]
        sine_part = twiddle[1, window, :]
        rows = pl.ds(pulse * RADIX, RADIX)
        twisted[rows, pl.ds(0, LANES)] = (real_part * cosine - imag_part * sine_part).astype(jnp.bfloat16)
        twisted[rows, pl.ds(LANES, LANES)] = (real_part * sine_part + imag_part * cosine).astype(jnp.bfloat16)
    row_index = lax.broadcasted_iota(jnp.int32, (RADIX, LANES), 0)
    lane_index = lax.broadcasted_iota(jnp.int32, (RADIX, LANES), 1)
    gates = row_index * LANES + lane_index
    for pulse in range(pulse_count):
        sums = lax.dot_general(
            second[...],
            twisted[pl.ds(pulse * RADIX, RADIX), :],
            (((1,), (1,)), ((), ())),
            preferred_element_type=jnp.float32,
        )
        inside = gates < SAMPLES - delays[pulse]
        real_part, imag_part = sums[:RADIX], sums[RADIX:]
        cosine, sine_part = near[0], near[1]
        turned[pl.ds(pulse, RADIX, stride=pulse_count), :] = jnp.where(
            inside, real_part * cosine - imag_part * sine_part, 0.0
        )
        turned[pl.ds(span + pulse, RADIX, stride=pulse_count), :] = jnp.where(
            inside, real_part * sine_part + imag_part * cosine, 0.0
        )
    for step in range(RADIX):
        block, column = divmod(step * LANES, width)
        rows = pl.ds(step * pulse_count, pulse_count)
        both = jnp.concatenate(
            [turned[rows, :], turned[pl.ds(span + step * pulse_count, pulse_count), :]], axis=0
        )
        out[block, :, pl.ds(column, LANES)] = both.astype(jnp.bfloat16)


def range_compress(raw_echo, delays, depth_count, sub_pulses, gate_count):
    pulse_count = raw_echo.shape[1]
    width = SAMPLES // gate_count
    span = RADIX * pulse_count
    dft = to_bf16(real_form(dft_table()))
    vmem = pl.BlockSpec(memory_space=pltpu.VMEM)
    return pl.pallas_call(
        compress_kernel,
        out_shape=jax.ShapeDtypeStruct((gate_count, 2 * pulse_count, width), jnp.bfloat16),
        in_specs=[pl.BlockSpec(memory_space=pltpu.SMEM)] + [vmem] * 5,
        out_specs=vmem,
        scratch_shapes=[
            pltpu.VMEM((2 * span, LANES), jnp.float32),
            pltpu.VMEM((2 * RADIX, pulse_count * LANES), jnp.bfloat16),
            pltpu.VMEM((pulse_count, 2, ROWS, LANES), jnp.float32),
            pltpu.VMEM((span, 2 * LANES), jnp.bfloat16),
            pltpu.VMEM((2 * span, LANES), jnp.float32),
        ],
        compiler_params=pltpu.CompilerParams(vmem_limit_bytes=32 * 2**20),
        name="compress",
    )(delays, raw_echo, dft, dft, twiddles(), near_phases(depth_count, sub_pulses))


def image_kernel(table, own, other, out):
    depth = own.shape[0]
    rows, columns = out.shape
    tile_rows, tile_columns = min(rows, 256), min(columns, 256)
    for row in range(0, rows, tile_rows):
        for column in range(0, columns, tile_columns):
            place = pl.ds(row, tile_rows), pl.ds(column, tile_columns)
            total = jnp.dot(
                table[place[0], pl.ds(0, depth)], own[:, place[1]], preferred_element_type=jnp.float32
            ) + jnp.dot(
                table[place[0], pl.ds(depth, depth)], other[:, place[1]], preferred_element_type=jnp.float32
            )
            out[place] = total.astype(jnp.bfloat16)


def form_image(table, own, other):
    vmem = pl.BlockSpec(memory_space=pltpu.VMEM)
    image = pl.pallas_call(
        image_kernel,
        out_shape=jax.ShapeDtypeStruct((2 * ANGLES, own.shape[1]), jnp.bfloat16),
        in_specs=[vmem] * 3,
        out_specs=vmem,
        compiler_params=pltpu.CompilerParams(vmem_limit_bytes=32 * 2**20),
        name="image",
    )(table, own, other)
    return image.reshape(2, ANGLES, own.shape[1])


def partner(array, axis, apart):
    return lax.ppermute(array, axis, [(i, i ^ 1 << apart) for i in range(lax.axis_size(axis))])


def merge_levels(received, pulse_count, sub_pulses, depth_count):
    half = ANGLES // 2
    sub_index = lax.axis_index("sub")
    steering = to_bf16(by_source(real_form(steer_table(sub_pulses)), pulse_count))
    current = jnp.dot(steering, received, preferred_element_type=jnp.float32).astype(jnp.bfloat16)
    current = current.reshape(2, ANGLES, -1)
    sector = jnp.zeros((), jnp.int32)
    interp = jnp.asarray(interp_table(), jnp.float32)
    for depth in range(1, depth_count + 1):
        side_bit = sub_index // 2 ** (depth - 1) % 2
        sent = lax.dynamic_slice_in_dim(current, (1 - side_bit) * half, half, axis=1)
        kept = lax.dynamic_slice_in_dim(current, side_bit * half, half, axis=1)
        arrived = partner(sent, "sub", depth - 1)
        sector = 2 * sector + side_bit
        modulus = ANGLES * 2 ** (depth + 3)
        numerator = 2 * (sector * ANGLES + jnp.arange(ANGLES, dtype=jnp.int32)) + 1 - ANGLES * 2**depth
        center = (2 * side_bit - 1) * (sub_pulses * 2 ** (depth - 1) // 2)
        total = 0.0
        for child, place in ((kept, center), (arrived, -center)):
            turns = jnp.mod(place * numerator, modulus).astype(jnp.float32) / modulus
            cosine = (jnp.cos(TWO_PI * turns) * math.sqrt(0.5))[:, None] * interp
            sine_part = (-jnp.sin(TWO_PI * turns) * math.sqrt(0.5))[:, None] * interp
            table = jnp.stack([jnp.stack([cosine, -sine_part]), jnp.stack([sine_part, cosine])])
            total = total + jnp.einsum(
                "akjh,khg->ajg", table.astype(jnp.bfloat16), child, preferred_element_type=jnp.float32
            )
        current = total.astype(jnp.bfloat16)
    return current


def per_device(raw_echo, delays):
    gate_count = lax.axis_size("gate")
    sub_count = lax.axis_size("sub")
    pulse_count = raw_echo.shape[1]
    sub_pulses = pulse_count * gate_count
    depth_count = sub_count.bit_length() - 1
    compressed = range_compress(raw_echo, delays, depth_count, sub_pulses, gate_count)
    received = lax.all_to_all(compressed, "gate", split_axis=0, concat_axis=0, tiled=True)
    received = received.reshape(2 * sub_pulses, SAMPLES // gate_count)
    if depth_count != 1:
        return merge_levels(received, pulse_count, sub_pulses, depth_count)
    other = partner(received, "sub", 0)
    tables = jnp.asarray(image_tables(sub_pulses, pulse_count))
    table = lax.dynamic_index_in_dim(tables, lax.axis_index("sub"), 0, keepdims=False)
    return form_image(table, received, other)


def solution(mesh):
    placed = (P(None, ("sub", "gate"), None), P(("sub", "gate")))
    return jax.shard_map(
        per_device, mesh=mesh, in_specs=placed, out_specs=P(None, "sub", "gate"), check_vma=False
    )
```

```python
import functools
import math

import jax
import jax.numpy as jnp
import numpy as np
from jax import lax
from jax.experimental import pallas as pl
from jax.experimental.pallas import tpu as pltpu
from jax.sharding import PartitionSpec as P

RADIX = 128
SAMPLES = 16384
ANGLES = 256
DELAY_MAX = 64
LANES = 128
RAW_PIECES = 4
ROWS = RADIX + DELAY_MAX


TWO_PI = 2.0 * math.pi


def to_bf16(values):
    return np.asarray(values, np.float32).astype(jnp.bfloat16)


def rounded(values):
    return to_bf16(values).astype(np.float64)


def real_form(table):
    upper = np.concatenate([table.real, -table.imag], axis=1)
    lower = np.concatenate([table.imag, table.real], axis=1)
    return np.concatenate([upper, lower], axis=0)


def unit(phases):
    return np.cos(phases) + 1j * np.sin(phases)


def dft_table():
    counter = np.arange(RADIX)
    table = unit(-TWO_PI / RADIX * (counter[:, None] * counter[None, :] % RADIX)) / math.sqrt(RADIX)
    return rounded(table.real) + 1j * rounded(table.imag)


def twiddles():
    phases = -TWO_PI / SAMPLES * (np.arange(ROWS)[:, None] * np.arange(RADIX)[None, :])
    return np.stack([np.cos(phases), np.sin(phases)]).astype(np.float32)


def near_phases(depth_count, sub_pulses):
    centers = [sub_pulses * 2 ** (depth - 1) // 2 for depth in range(1, depth_count + 1)]
    center_sq = float(sum(center * center for center in centers))
    phases = -TWO_PI / (4 * ANGLES) * center_sq / (16.0 * (SAMPLES + np.arange(SAMPLES)))
    return np.stack([np.cos(phases), np.sin(phases)]).astype(np.float32).reshape(2, RADIX, RADIX)


def steer_table(sub_pulses):
    modulus = 16 * ANGLES
    beams = 2 * np.arange(ANGLES) - ANGLES + 1
    pulses = 2 * np.arange(sub_pulses) - sub_pulses + 1
    table = unit(-TWO_PI / modulus * (beams[:, None] * pulses[None, :] % modulus)) / math.sqrt(sub_pulses)
    return rounded(table.real) + 1j * rounded(table.imag)


def interp_table():
    distance = np.arange(ANGLES)[:, None] * 0.5 - 0.25 - np.arange(ANGLES // 2)[None, :]
    taper = np.where(np.abs(distance) < 4.0, 0.5 + 0.5 * np.cos(math.pi * distance / 4.0), 0.0)
    return rounded(np.sinc(distance) * taper)


def merge_table(depth, sector, center):
    modulus = ANGLES * 2 ** (depth + 3)
    row_index = sector * ANGLES + np.arange(ANGLES)
    numerator = 2 * row_index + 1 - ANGLES * 2**depth
    turns = (center * numerator) % modulus / modulus
    return unit(-TWO_PI * turns)[:, None] * interp_table() / math.sqrt(2.0)


def by_source(table, pulse_count):
    rows = table.shape[0]
    return table.reshape(rows, 2, -1, pulse_count).transpose(0, 2, 1, 3).reshape(rows, -1)


def image_tables(sub_pulses, pulse_count):
    half = ANGLES // 2
    steer = steer_table(sub_pulses)
    tables = []
    for sub in range(2):
        beams = steer[sub * half : (sub + 1) * half]
        own = (2 * sub - 1) * (sub_pulses // 2)
        parts = [real_form(merge_table(1, sub, center) @ beams) for center in (own, -own)]
        tables.append(np.concatenate([by_source(part, pulse_count) for part in parts], axis=1))
    return to_bf16(np.stack(tables))


def compress_kernel(
    plan, delays, raw_far, dft_far, twiddle_far, near_far, *refs
):
    outs = refs[: len(plan)]
    (
    raw, dft, twiddle, near, arrived, lines, grid_in, section, twisted, turned,
    ) = refs[len(plan) :]
    pulse_count = raw.shape[1]
    width = outs[0].shape[-1]
    me = lax.axis_index("gate")
    span = RADIX * pulse_count
    piece = SAMPLES // RAW_PIECES
    pieces = [
        pltpu.make_async_copy(
            raw_far.at[:, :, pl.ds(index * piece, piece)],
            raw.at[:, :, pl.ds(index * piece, piece)],
            arrived.at[index],
        )
        for index in range(RAW_PIECES)
    ]
    tables = [
        pltpu.make_async_copy(far, here, arrived.at[RAW_PIECES + index])
        for index, (far, here) in enumerate(((dft_far, dft), (twiddle_far, twiddle), (near_far, near)))
    ]
    for copy in pieces + tables:
        copy.start()
    for step in range(RADIX):
        if step * LANES % piece == 0:
            pieces[step * LANES // piece].wait()
        for part in range(2):
            lines[pl.ds(part * span + step * pulse_count, pulse_count), :] = raw[
                part, :, pl.ds(step * LANES, LANES)
            ].astype(jnp.float32)
    for part in range(2):
        for pulse in range(pulse_count):
            grid_in[pl.ds(part * RADIX, RADIX), pl.ds(pulse * LANES, LANES)] = lines[
                pl.ds(part * span + pulse, RADIX, stride=pulse_count), :
            ].astype(jnp.bfloat16)
    tables[0].wait()
    for pulse in range(pulse_count):
        columns = pl.ds(pulse * LANES, LANES)
        sums = jnp.dot(dft[...], grid_in[:, columns], preferred_element_type=jnp.float32)
        for part in range(2):
            own = sums[part * RADIX : (part + 1) * RADIX]
            section[pulse, part, pl.ds(0, RADIX), :] = own
            section[pulse, part, pl.ds(RADIX, DELAY_MAX), :] = own[:DELAY_MAX]
    tables[1].wait()
    for pulse in range(pulse_count):
        window = pl.ds(delays[pulse], RADIX)
        real_part = section[pulse, 0, window, :]
        imag_part = section[pulse, 1, window, :]
        cosine = twiddle[0, window, :]
        sine_part = twiddle[1, window, :]
        rows = pl.ds(pulse * RADIX, RADIX)
        twisted[rows, pl.ds(0, LANES)] = (real_part * cosine - imag_part * sine_part).astype(jnp.bfloat16)
        twisted[rows, pl.ds(LANES, LANES)] = (real_part * sine_part + imag_part * cosine).astype(jnp.bfloat16)
    row_index = lax.broadcasted_iota(jnp.int32, (RADIX, LANES), 0)
    lane_index = lax.broadcasted_iota(jnp.int32, (RADIX, LANES), 1)
    gates = row_index * LANES + lane_index
    tables[2].wait()
    for pulse in range(pulse_count):
        sums = lax.dot_general(
            dft[...],
            twisted[pl.ds(pulse * RADIX, RADIX), :],
            (((1,), (1,)), ((), ())),
            preferred_element_type=jnp.float32,
        )
        inside = gates < SAMPLES - delays[pulse]
        real_part, imag_part = sums[:RADIX], sums[RADIX:]
        cosine, sine_part = near[0], near[1]
        turned[pl.ds(pulse, RADIX, stride=pulse_count), :] = jnp.where(
            inside, real_part * cosine - imag_part * sine_part, 0.0
        )
        turned[pl.ds(span + pulse, RADIX, stride=pulse_count), :] = jnp.where(
            inside, real_part * sine_part + imag_part * cosine, 0.0
        )
    block_rows = width // LANES * pulse_count
    for out, places in zip(outs, plan, strict=True):
        for index, apart in enumerate(places):
            start = pl.multiple_of((me ^ apart) * block_rows, block_rows)
            for step in range(width // LANES):
                rows = pl.ds(start + step * pulse_count, pulse_count)
                both = jnp.concatenate([turned[rows, :], turned[pl.ds(span + start + step * pulse_count, pulse_count), :]], axis=0)
                out[index, :, pl.ds(step * LANES, LANES)] = both.astype(jnp.bfloat16)


def range_compress(raw_echo, delays, depth_count, sub_pulses, plan):
    gate_count = lax.axis_size("gate")
    pulse_count = raw_echo.shape[1]
    width = SAMPLES // gate_count
    span = RADIX * pulse_count
    dft = to_bf16(real_form(dft_table()))
    twiddle, near = twiddles(), near_phases(depth_count, sub_pulses)
    return pl.pallas_call(
        functools.partial(compress_kernel, plan),
        out_shape=[
            pltpu.VMEM((len(places), 2 * pulse_count, width), jnp.bfloat16) for places in plan
        ],
        in_specs=[pl.BlockSpec(memory_space=pltpu.SMEM)] + [pl.BlockSpec(memory_space=pltpu.HBM)] * 4,
        out_specs=[pl.BlockSpec(memory_space=pltpu.VMEM)] * len(plan),
        scratch_shapes=[
            pltpu.VMEM(raw_echo.shape, raw_echo.dtype),
            pltpu.VMEM(dft.shape, dft.dtype),
            pltpu.VMEM(twiddle.shape, twiddle.dtype),
            pltpu.VMEM(near.shape, near.dtype),
            pltpu.SemaphoreType.DMA((RAW_PIECES + 3,)),
            pltpu.VMEM((2 * span, LANES), jnp.float32),
            pltpu.VMEM((2 * RADIX, pulse_count * LANES), jnp.bfloat16),
            pltpu.VMEM((pulse_count, 2, ROWS, LANES), jnp.float32),
            pltpu.VMEM((span, 2 * LANES), jnp.bfloat16),
            pltpu.VMEM((2 * span, LANES), jnp.float32),
        ],
        compiler_params=pltpu.CompilerParams(vmem_limit_bytes=60 * 2**20),
        name="compress",
    )(delays, raw_echo, dft, twiddle, near)


def image_kernel(plan, table, *refs):
    arrays, (out, data) = refs[: len(plan)], refs[len(plan) :]
    rows, columns = out.shape
    depth = data.shape[0]
    block = arrays[0].shape[1]
    me = lax.axis_index("gate")
    for array, (side, places) in zip(arrays, plan, strict=True):
        for index, apart in enumerate(places):
            start = pl.multiple_of(side * (depth // 2) + (me ^ apart) * block, block)
            data[pl.ds(start, block), :] = array[index]
    tile_rows, tile_columns = min(rows, 256), min(columns, 256)
    for row in range(0, rows, tile_rows):
        for column in range(0, columns, tile_columns):
            place = pl.ds(row, tile_rows), pl.ds(column, tile_columns)
            out[place] = jnp.dot(
                table[place[0], :], data[:, place[1]], preferred_element_type=jnp.float32
            ).astype(jnp.bfloat16)


def form_image(table, arrays, plan):
    vmem = pl.BlockSpec(memory_space=pltpu.VMEM)
    width = arrays[0].shape[-1]
    image = pl.pallas_call(
        functools.partial(image_kernel, plan),
        out_shape=jax.ShapeDtypeStruct((2 * ANGLES, width), jnp.bfloat16),
        in_specs=[vmem] * (1 + len(arrays)),
        out_specs=vmem,
        scratch_shapes=[pltpu.VMEM((table.shape[1], width), jnp.bfloat16)],
        compiler_params=pltpu.CompilerParams(vmem_limit_bytes=32 * 2**20),
        name="image",
    )(table, *arrays)
    return image.reshape(2, ANGLES, width)


def partner(array, axis, apart):
    return lax.ppermute(array, axis, [(i, i ^ 1 << apart) for i in range(lax.axis_size(axis))])


def merge_levels(received, pulse_count, sub_pulses, depth_count):
    half = ANGLES // 2
    sub_index = lax.axis_index("sub")
    steering = to_bf16(by_source(real_form(steer_table(sub_pulses)), pulse_count))
    current = jnp.dot(steering, received, preferred_element_type=jnp.float32).astype(jnp.bfloat16)
    current = current.reshape(2, ANGLES, -1)
    sector = jnp.zeros((), jnp.int32)
    interp = jnp.asarray(interp_table(), jnp.float32)
    for depth in range(1, depth_count + 1):
        side_bit = sub_index // 2 ** (depth - 1) % 2
        sent = lax.dynamic_slice_in_dim(current, (1 - side_bit) * half, half, axis=1)
        kept = lax.dynamic_slice_in_dim(current, side_bit * half, half, axis=1)
        arrived = partner(sent, "sub", depth - 1)
        sector = 2 * sector + side_bit
        modulus = ANGLES * 2 ** (depth + 3)
        numerator = 2 * (sector * ANGLES + jnp.arange(ANGLES, dtype=jnp.int32)) + 1 - ANGLES * 2**depth
        center = (2 * side_bit - 1) * (sub_pulses * 2 ** (depth - 1) // 2)
        total = 0.0
        for child, place in ((kept, center), (arrived, -center)):
            turns = jnp.mod(place * numerator, modulus).astype(jnp.float32) / modulus
            cosine = (jnp.cos(TWO_PI * turns) * math.sqrt(0.5))[:, None] * interp
            sine_part = (-jnp.sin(TWO_PI * turns) * math.sqrt(0.5))[:, None] * interp
            table = jnp.stack([jnp.stack([cosine, -sine_part]), jnp.stack([sine_part, cosine])])
            total = total + jnp.einsum(
                "akjh,khg->ajg", table.astype(jnp.bfloat16), child, preferred_element_type=jnp.float32
            )
        current = total.astype(jnp.bfloat16)
    return current


def swap(array, apart, other_sub=False):
    count = lax.axis_size("gate")
    if not other_sub:
        return lax.ppermute(array, "gate", [(i, i ^ apart) for i in range(count)])
    pairs = [(i, i ^ (count + apart)) for i in range(2 * count)]
    return lax.ppermute(array, ("sub", "gate"), pairs)


CORE, Y, Z = 1, 2, 4


def corner_turn(send):
    near, far = [0, Y], [CORE, CORE | Y]
    plan = [near, [Z + i for i in near], [2 * Z + i for i in near], [3 * Z + i for i in near]]
    plan.append([k * Z + i for k in range(4) for i in far])
    own = send(plan)
    mate = swap(own[4], CORE).reshape((4,) + own[0].shape)
    both = [jnp.stack(pair, axis=1) for pair in zip(own[:4], mate, strict=True)]
    moved = both[:1] + [swap(both[k], k * Z) for k in range(1, 4)]
    groups = [moved[:2], moved[2:]]
    arrays, places = [], []
    for index, pair in enumerate(groups):
        home = jnp.concatenate([half[0] for half in pair])
        away = jnp.concatenate([half[1] for half in pair])
        apart = [k * Z + core for k in (2 * index, 2 * index + 1) for core in (0, CORE)]
        apart_y = [i + Y for i in apart]
        arrays += [home, swap(away, Y, True), swap(home, 0, True), swap(away, Y)]
        places += [(0, apart), (1, apart_y), (1, apart), (0, apart_y)]
    return arrays, places


def per_device(raw_echo, delays):
    gate_count = lax.axis_size("gate")
    sub_count = lax.axis_size("sub")
    pulse_count = raw_echo.shape[1]
    sub_pulses = pulse_count * gate_count
    depth_count = sub_count.bit_length() - 1
    send = functools.partial(range_compress, raw_echo, delays, depth_count, sub_pulses)
    if (sub_count, gate_count) != (2, 16):
        (compressed,) = send([range(gate_count)])
        me = lax.axis_index("gate")
        ordered = compressed[me ^ jnp.arange(gate_count)]
        received = lax.all_to_all(ordered, "gate", split_axis=0, concat_axis=0, tiled=True)
        received = received.reshape(2 * sub_pulses, SAMPLES // gate_count)
        return merge_levels(received, pulse_count, sub_pulses, depth_count)
    arrays, places = corner_turn(send)
    tables = jnp.asarray(image_tables(sub_pulses, pulse_count))
    table = lax.dynamic_index_in_dim(tables, lax.axis_index("sub"), 0, keepdims=False)
    return form_image(table, arrays, places)


def solution(mesh):
    placed = (P(None, ("sub", "gate"), None), P(("sub", "gate")))
    return jax.shard_map(
        per_device, mesh=mesh, in_specs=placed, out_specs=P(None, "sub", "gate"), check_vma=False
    )
```

```python
import functools
import math

import jax
import jax.numpy as jnp
import numpy as np
from jax import lax
from jax.experimental import pallas as pl
from jax.experimental.pallas import tpu as pltpu
from jax.sharding import PartitionSpec as P

RADIX = 128
SAMPLES = 16384
ANGLES = 256
DELAY_MAX = 64
LANES = 128
RAW_PIECES = 4
ROWS = RADIX + DELAY_MAX


TWO_PI = 2.0 * math.pi


def to_bf16(values):
    return np.asarray(values, np.float32).astype(jnp.bfloat16)


def rounded(values):
    return to_bf16(values).astype(np.float64)


def real_form(table):
    upper = np.concatenate([table.real, -table.imag], axis=1)
    lower = np.concatenate([table.imag, table.real], axis=1)
    return np.concatenate([upper, lower], axis=0)


def unit(phases):
    return np.cos(phases) + 1j * np.sin(phases)


def dft_table():
    counter = np.arange(RADIX)
    table = unit(-TWO_PI / RADIX * (counter[:, None] * counter[None, :] % RADIX)) / math.sqrt(RADIX)
    return rounded(table.real) + 1j * rounded(table.imag)


def twiddles():
    phases = -TWO_PI / SAMPLES * (np.arange(ROWS)[:, None] * np.arange(RADIX)[None, :])
    return np.stack([np.cos(phases), np.sin(phases)]).astype(np.float32)


def near_phases(depth_count, sub_pulses):
    centers = [sub_pulses * 2 ** (depth - 1) // 2 for depth in range(1, depth_count + 1)]
    center_sq = float(sum(center * center for center in centers))
    phases = -TWO_PI / (4 * ANGLES) * center_sq / (16.0 * (SAMPLES + np.arange(SAMPLES)))
    return np.stack([np.cos(phases), np.sin(phases)]).astype(np.float32).reshape(2, RADIX, RADIX)


def steer_table(sub_pulses):
    modulus = 16 * ANGLES
    beams = 2 * np.arange(ANGLES) - ANGLES + 1
    pulses = 2 * np.arange(sub_pulses) - sub_pulses + 1
    table = unit(-TWO_PI / modulus * (beams[:, None] * pulses[None, :] % modulus)) / math.sqrt(sub_pulses)
    return rounded(table.real) + 1j * rounded(table.imag)


def interp_table():
    distance = np.arange(ANGLES)[:, None] * 0.5 - 0.25 - np.arange(ANGLES // 2)[None, :]
    taper = np.where(np.abs(distance) < 4.0, 0.5 + 0.5 * np.cos(math.pi * distance / 4.0), 0.0)
    return rounded(np.sinc(distance) * taper)


def merge_table(depth, sector, center):
    modulus = ANGLES * 2 ** (depth + 3)
    row_index = sector * ANGLES + np.arange(ANGLES)
    numerator = 2 * row_index + 1 - ANGLES * 2**depth
    turns = (center * numerator) % modulus / modulus
    return unit(-TWO_PI * turns)[:, None] * interp_table() / math.sqrt(2.0)


def by_source(table, pulse_count):
    rows = table.shape[0]
    return table.reshape(rows, 2, -1, pulse_count).transpose(0, 2, 1, 3).reshape(rows, -1)


def image_tables(sub_pulses, pulse_count):
    half = ANGLES // 2
    steer = steer_table(sub_pulses)
    tables = []
    for sub in range(2):
        beams = steer[sub * half : (sub + 1) * half]
        own = (2 * sub - 1) * (sub_pulses // 2)
        parts = [real_form(merge_table(1, sub, center) @ beams) for center in (own, -own)]
        tables.append(np.concatenate([by_source(part, pulse_count) for part in parts], axis=1))
    return to_bf16(np.stack(tables))


def compress_kernel(
    plan, delays, raw_far, dft_far, twiddle_far, near_far, *refs
):
    outs = refs[: len(plan)]
    (
    raw, dft, twiddle, near, arrived, lines, grid_in, section, twisted, turned,
    ) = refs[len(plan) :]
    pulse_count = raw.shape[1]
    width = outs[0].shape[-1]
    me = lax.axis_index("gate")
    span = RADIX * pulse_count
    piece = SAMPLES // RAW_PIECES
    pieces = [
        pltpu.make_async_copy(
            raw_far.at[:, :, pl.ds(index * piece, piece)],
            raw.at[:, :, pl.ds(index * piece, piece)],
            arrived.at[index],
        )
        for index in range(RAW_PIECES)
    ]
    tables = [
        pltpu.make_async_copy(far, here, arrived.at[RAW_PIECES + index])
        for index, (far, here) in enumerate(((dft_far, dft), (twiddle_far, twiddle), (near_far, near)))
    ]
    for copy in pieces + tables:
        copy.start()
    for step in range(RADIX):
        if step * LANES % piece == 0:
            pieces[step * LANES // piece].wait()
        for part in range(2):
            lines[pl.ds(part * span + step * pulse_count, pulse_count), :] = raw[
                part, :, pl.ds(step * LANES, LANES)
            ].astype(jnp.float32)
    for part in range(2):
        for pulse in range(pulse_count):
            grid_in[pl.ds(part * RADIX, RADIX), pl.ds(pulse * LANES, LANES)] = lines[
                pl.ds(part * span + pulse, RADIX, stride=pulse_count), :
            ].astype(jnp.bfloat16)
    tables[0].wait()
    for pulse in range(pulse_count):
        columns = pl.ds(pulse * LANES, LANES)
        sums = jnp.dot(dft[...], grid_in[:, columns], preferred_element_type=jnp.float32)
        for part in range(2):
            own = sums[part * RADIX : (part + 1) * RADIX]
            section[pulse, part, pl.ds(0, RADIX), :] = own
            section[pulse, part, pl.ds(RADIX, DELAY_MAX), :] = own[:DELAY_MAX]
    tables[1].wait()
    for pulse in range(pulse_count):
        window = pl.ds(delays[pulse], RADIX)
        real_part = section[pulse, 0, window, :]
        imag_part = section[pulse, 1, window, :]
        cosine = twiddle[0, window, :]
        sine_part = twiddle[1, window, :]
        rows = pl.ds(pulse * RADIX, RADIX)
        twisted[rows, pl.ds(0, LANES)] = (real_part * cosine - imag_part * sine_part).astype(jnp.bfloat16)
        twisted[rows, pl.ds(LANES, LANES)] = (real_part * sine_part + imag_part * cosine).astype(jnp.bfloat16)
    row_index = lax.broadcasted_iota(jnp.int32, (RADIX, LANES), 0)
    lane_index = lax.broadcasted_iota(jnp.int32, (RADIX, LANES), 1)
    gates = row_index * LANES + lane_index
    tables[2].wait()
    for pulse in range(pulse_count):
        sums = lax.dot_general(
            dft[...],
            twisted[pl.ds(pulse * RADIX, RADIX), :],
            (((1,), (1,)), ((), ())),
            preferred_element_type=jnp.float32,
        )
        inside = gates < SAMPLES - delays[pulse]
        real_part, imag_part = sums[:RADIX], sums[RADIX:]
        cosine, sine_part = near[0], near[1]
        turned[pl.ds(pulse, RADIX, stride=pulse_count), :] = jnp.where(
            inside, real_part * cosine - imag_part * sine_part, 0.0
        )
        turned[pl.ds(span + pulse, RADIX, stride=pulse_count), :] = jnp.where(
            inside, real_part * sine_part + imag_part * cosine, 0.0
        )
    block_rows = width // LANES * pulse_count
    for out, places in zip(outs, plan, strict=True):
        for index, apart in enumerate(places):
            start = pl.multiple_of((me ^ apart) * block_rows, block_rows)
            for step in range(width // LANES):
                rows = pl.ds(start + step * pulse_count, pulse_count)
                both = jnp.concatenate([turned[rows, :], turned[pl.ds(span + start + step * pulse_count, pulse_count), :]], axis=0)
                out[index, :, pl.ds(step * LANES, LANES)] = both.astype(jnp.bfloat16)


def range_compress(raw_echo, delays, depth_count, sub_pulses, plan):
    gate_count = lax.axis_size("gate")
    pulse_count = raw_echo.shape[1]
    width = SAMPLES // gate_count
    span = RADIX * pulse_count
    dft = to_bf16(real_form(dft_table()))
    twiddle, near = twiddles(), near_phases(depth_count, sub_pulses)
    return pl.pallas_call(
        functools.partial(compress_kernel, plan),
        out_shape=[
            pltpu.VMEM((len(places), 2 * pulse_count, width), jnp.bfloat16) for places in plan
        ],
        in_specs=[pl.BlockSpec(memory_space=pltpu.SMEM)] + [pl.BlockSpec(memory_space=pltpu.HBM)] * 4,
        out_specs=[pl.BlockSpec(memory_space=pltpu.VMEM)] * len(plan),
        scratch_shapes=[
            pltpu.VMEM(raw_echo.shape, raw_echo.dtype),
            pltpu.VMEM(dft.shape, dft.dtype),
            pltpu.VMEM(twiddle.shape, twiddle.dtype),
            pltpu.VMEM(near.shape, near.dtype),
            pltpu.SemaphoreType.DMA((RAW_PIECES + 3,)),
            pltpu.VMEM((2 * span, LANES), jnp.float32),
            pltpu.VMEM((2 * RADIX, pulse_count * LANES), jnp.bfloat16),
            pltpu.VMEM((pulse_count, 2, ROWS, LANES), jnp.float32),
            pltpu.VMEM((span, 2 * LANES), jnp.bfloat16),
            pltpu.VMEM((2 * span, LANES), jnp.float32),
        ],
        compiler_params=pltpu.CompilerParams(vmem_limit_bytes=60 * 2**20),
        name="compress",
    )(delays, raw_echo, dft, twiddle, near)


def image_kernel(plan, far, has_total, table, *refs):
    arrays, refs = refs[: len(plan)], refs[len(plan) :]
    total, (out, data, columns) = (refs[0], refs[1:]) if has_total else (None, refs)
    half = data.shape[0] // 2
    block = arrays[0].shape[1]
    me = lax.axis_index("gate")
    lower = (me ^ far) // FAR * half
    for array, (side, places) in zip(arrays, plan, strict=True):
        for index, apart in enumerate(places):
            if apart // FAR * FAR == far:
                start = side * half + (me ^ apart) * block - lower
                data[pl.ds(pl.multiple_of(start, block), block), :] = array[index]
    for side in range(2):
        source = pl.multiple_of(side * 2 * half + lower, half)
        columns[:, pl.ds(side * half, half)] = table[:, pl.ds(source, half)]
    tile = 256
    for row in range(0, out.shape[0], tile):
        for column in range(0, out.shape[1], tile):
            place = pl.ds(row, tile), pl.ds(column, tile)
            sums = jnp.dot(columns[place[0], :], data[:, place[1]], preferred_element_type=jnp.float32)
            if has_total:
                sums = sums + total[place]
            out[place] = sums.astype(out.dtype)


def form_image(table, arrays, plan):
    rows, depth = table.shape[0], table.shape[1] // 2
    shape = rows, arrays[0].shape[-1]
    vmem = pl.BlockSpec(memory_space=pltpu.VMEM)
    total = []
    for far in (0, FAR):
        used = [i for i, (_, places) in enumerate(plan) if any(apart // FAR * FAR == far for apart in places)]
        image = pl.pallas_call(
            functools.partial(image_kernel, [plan[i] for i in used], far, bool(total)),
            out_shape=jax.ShapeDtypeStruct(shape, jnp.bfloat16) if far else pltpu.VMEM(shape, jnp.float32),
            in_specs=[vmem] * (1 + len(used) + len(total)),
            out_specs=vmem,
            scratch_shapes=[pltpu.VMEM((depth, shape[1]), jnp.bfloat16), pltpu.VMEM((rows, depth), jnp.bfloat16)],
            cost_estimate=pl.CostEstimate(
                flops=2 * depth * math.prod(shape), bytes_accessed=4 * math.prod(shape), transcendentals=0
            ),
            compiler_params=pltpu.CompilerParams(vmem_limit_bytes=32 * 2**20),
            name="image",
        )(table, *[arrays[i] for i in used], *total)
        total = [image]
    return image.reshape(2, ANGLES, shape[1])


def partner(array, axis, apart):
    return lax.ppermute(array, axis, [(i, i ^ 1 << apart) for i in range(lax.axis_size(axis))])


def merge_levels(received, pulse_count, sub_pulses, depth_count):
    half = ANGLES // 2
    sub_index = lax.axis_index("sub")
    steering = to_bf16(by_source(real_form(steer_table(sub_pulses)), pulse_count))
    current = jnp.dot(steering, received, preferred_element_type=jnp.float32).astype(jnp.bfloat16)
    current = current.reshape(2, ANGLES, -1)
    sector = jnp.zeros((), jnp.int32)
    interp = jnp.asarray(interp_table(), jnp.float32)
    for depth in range(1, depth_count + 1):
        side_bit = sub_index // 2 ** (depth - 1) % 2
        sent = lax.dynamic_slice_in_dim(current, (1 - side_bit) * half, half, axis=1)
        kept = lax.dynamic_slice_in_dim(current, side_bit * half, half, axis=1)
        arrived = partner(sent, "sub", depth - 1)
        sector = 2 * sector + side_bit
        modulus = ANGLES * 2 ** (depth + 3)
        numerator = 2 * (sector * ANGLES + jnp.arange(ANGLES, dtype=jnp.int32)) + 1 - ANGLES * 2**depth
        center = (2 * side_bit - 1) * (sub_pulses * 2 ** (depth - 1) // 2)
        total = 0.0
        for child, place in ((kept, center), (arrived, -center)):
            turns = jnp.mod(place * numerator, modulus).astype(jnp.float32) / modulus
            cosine = (jnp.cos(TWO_PI * turns) * math.sqrt(0.5))[:, None] * interp
            sine_part = (-jnp.sin(TWO_PI * turns) * math.sqrt(0.5))[:, None] * interp
            table = jnp.stack([jnp.stack([cosine, -sine_part]), jnp.stack([sine_part, cosine])])
            total = total + jnp.einsum(
                "akjh,khg->ajg", table.astype(jnp.bfloat16), child, preferred_element_type=jnp.float32
            )
        current = total.astype(jnp.bfloat16)
    return current


def swap(array, apart, other_sub=False):
    count = lax.axis_size("gate")
    if not other_sub:
        return lax.ppermute(array, "gate", [(i, i ^ apart) for i in range(count)])
    pairs = [(i, i ^ (count + apart)) for i in range(2 * count)]
    return lax.ppermute(array, ("sub", "gate"), pairs)


CORE, Y, Z, FAR = 1, 2, 4, 8


def after(array, other):
    return lax.optimization_barrier((array, other))[0]


def corner_turn(send):
    plan = [[place * Z, place * Z + Y] for place in range(4)]
    plan.append([place * Z + CORE + y for place in (0, 1, 3) for y in (0, Y)])
    plan.append([2 * Z + CORE, 2 * Z + CORE + Y])
    here, one, two, three, mates, mates_two = send(plan)
    width = here.shape[-1]
    mates = swap(mates, CORE)
    mates_two = swap(after(mates_two, mates), CORE)
    mates = mates.reshape(3, 2, -1, width)
    two = swap(two, 2 * Z)
    one = swap(jnp.stack([one, mates[1]], axis=1), Z)
    three = swap(jnp.stack([three, mates[2]], axis=1), 3 * Z)
    mates_two = swap(mates_two, 2 * Z)
    two = after(two, one)
    here = jnp.stack([here, mates[0]], axis=1)
    two = jnp.stack([two, mates_two], axis=1)
    near = [0, CORE, Z, Z + CORE]
    groups = [
        ([here[0], one[0]], [here[1], one[1]], near),
        ([two[0], three[0]], [two[1], three[1]], [FAR + i for i in near]),
    ]
    arrays, places = [], []
    for home, away, apart in groups:
        home, away = jnp.concatenate(home), jnp.concatenate(away)
        apart_y = [i + Y for i in apart]
        arrays += [home, swap(away, Y, True), swap(home, 0, True), swap(away, Y)]
        places += [(0, apart), (1, apart_y), (1, apart), (0, apart_y)]
    return arrays, places


def per_device(raw_echo, delays):
    gate_count = lax.axis_size("gate")
    sub_count = lax.axis_size("sub")
    pulse_count = raw_echo.shape[1]
    sub_pulses = pulse_count * gate_count
    depth_count = sub_count.bit_length() - 1
    send = functools.partial(range_compress, raw_echo, delays, depth_count, sub_pulses)
    if (sub_count, gate_count) != (2, 16):
        (compressed,) = send([range(gate_count)])
        me = lax.axis_index("gate")
        ordered = compressed[me ^ jnp.arange(gate_count)]
        received = lax.all_to_all(ordered, "gate", split_axis=0, concat_axis=0, tiled=True)
        received = received.reshape(2 * sub_pulses, SAMPLES // gate_count)
        return merge_levels(received, pulse_count, sub_pulses, depth_count)
    arrays, places = corner_turn(send)
    tables = jnp.asarray(image_tables(sub_pulses, pulse_count))
    table = lax.dynamic_index_in_dim(tables, lax.axis_index("sub"), 0, keepdims=False)
    return form_image(table, arrays, places)


def solution(mesh):
    placed = (P(None, ("sub", "gate"), None), P(("sub", "gate")))
    return jax.shard_map(
        per_device, mesh=mesh, in_specs=placed, out_specs=P(None, "sub", "gate"), check_vma=False
    )
```

```python
import functools
import math

import jax
import jax.numpy as jnp
import numpy as np
from jax import lax
from jax.experimental import pallas as pl
from jax.experimental.pallas import tpu as pltpu
from jax.sharding import PartitionSpec as P

RADIX = 128
SAMPLES = 16384
ANGLES = 256
DELAY_MAX = 64
LANES = 128
RAW_PIECES = 4
ROWS = RADIX + DELAY_MAX


TWO_PI = 2.0 * math.pi


def to_bf16(values):
    return np.asarray(values, np.float32).astype(jnp.bfloat16)


def rounded(values):
    return to_bf16(values).astype(np.float64)


def real_form(table):
    upper = np.concatenate([table.real, -table.imag], axis=1)
    lower = np.concatenate([table.imag, table.real], axis=1)
    return np.concatenate([upper, lower], axis=0)


def unit(phases):
    return np.cos(phases) + 1j * np.sin(phases)


def dft_table():
    counter = np.arange(RADIX)
    table = unit(-TWO_PI / RADIX * (counter[:, None] * counter[None, :] % RADIX)) / math.sqrt(RADIX)
    return rounded(table.real) + 1j * rounded(table.imag)


def twiddles():
    phases = -TWO_PI / SAMPLES * (np.arange(ROWS)[:, None] * np.arange(RADIX)[None, :])
    return np.stack([np.cos(phases), np.sin(phases)]).astype(np.float32)


def near_phases(depth_count, sub_pulses):
    centers = [sub_pulses * 2 ** (depth - 1) // 2 for depth in range(1, depth_count + 1)]
    center_sq = float(sum(center * center for center in centers))
    phases = -TWO_PI / (4 * ANGLES) * center_sq / (16.0 * (SAMPLES + np.arange(SAMPLES)))
    return np.stack([np.cos(phases), np.sin(phases)]).astype(np.float32).reshape(2, RADIX, RADIX)


def steer_table(sub_pulses):
    modulus = 16 * ANGLES
    beams = 2 * np.arange(ANGLES) - ANGLES + 1
    pulses = 2 * np.arange(sub_pulses) - sub_pulses + 1
    table = unit(-TWO_PI / modulus * (beams[:, None] * pulses[None, :] % modulus)) / math.sqrt(sub_pulses)
    return rounded(table.real) + 1j * rounded(table.imag)


def interp_table():
    distance = np.arange(ANGLES)[:, None] * 0.5 - 0.25 - np.arange(ANGLES // 2)[None, :]
    taper = np.where(np.abs(distance) < 4.0, 0.5 + 0.5 * np.cos(math.pi * distance / 4.0), 0.0)
    return rounded(np.sinc(distance) * taper)


def merge_table(depth, sector, center):
    modulus = ANGLES * 2 ** (depth + 3)
    row_index = sector * ANGLES + np.arange(ANGLES)
    numerator = 2 * row_index + 1 - ANGLES * 2**depth
    turns = (center * numerator) % modulus / modulus
    return unit(-TWO_PI * turns)[:, None] * interp_table() / math.sqrt(2.0)


def by_source(table, pulse_count):
    rows = table.shape[0]
    return table.reshape(rows, 2, -1, pulse_count).transpose(0, 2, 1, 3).reshape(rows, -1)


def image_tables(sub_pulses, pulse_count):
    half = ANGLES // 2
    steer = steer_table(sub_pulses)
    tables = []
    for sub in range(2):
        beams = steer[sub * half : (sub + 1) * half]
        own = (2 * sub - 1) * (sub_pulses // 2)
        parts = [real_form(merge_table(1, sub, center) @ beams) for center in (own, -own)]
        tables.append(np.concatenate([by_source(part, pulse_count) for part in parts], axis=1))
    return to_bf16(np.stack(tables))


def compress_kernel(
    plan, delays_far, raw_far, dft_far, twiddle_far, near_far, *refs
):
    outs = refs[: len(plan)]
    (
    delays, raw, dft, twiddle, near, arrived, lines, grid_in, section, twisted, turned,
    ) = refs[len(plan) :]
    pulse_count = raw.shape[1]
    width = outs[0].shape[-1]
    me = lax.axis_index("gate")
    span = RADIX * pulse_count
    piece = SAMPLES // RAW_PIECES
    pieces = [
        pltpu.make_async_copy(
            raw_far.at[:, :, pl.ds(index * piece, piece)],
            raw.at[:, :, pl.ds(index * piece, piece)],
            arrived.at[index],
        )
        for index in range(RAW_PIECES)
    ]
    tables = [
        pltpu.make_async_copy(far, here, arrived.at[RAW_PIECES + index])
        for index, (far, here) in enumerate(
            ((dft_far, dft), (delays_far, delays), (twiddle_far, twiddle), (near_far, near))
        )
    ]
    for copy in pieces + tables:
        copy.start()
    for step in range(RADIX):
        if step * LANES % piece == 0:
            pieces[step * LANES // piece].wait()
        for part in range(2):
            lines[pl.ds(part * span + step * pulse_count, pulse_count), :] = raw[
                part, :, pl.ds(step * LANES, LANES)
            ].astype(jnp.float32)
    for part in range(2):
        for pulse in range(pulse_count):
            grid_in[pl.ds(part * RADIX, RADIX), pl.ds(pulse * LANES, LANES)] = lines[
                pl.ds(part * span + pulse, RADIX, stride=pulse_count), :
            ].astype(jnp.bfloat16)
    tables[0].wait()
    for pulse in range(pulse_count):
        columns = pl.ds(pulse * LANES, LANES)
        sums = jnp.dot(dft[...], grid_in[:, columns], preferred_element_type=jnp.float32)
        for part in range(2):
            own = sums[part * RADIX : (part + 1) * RADIX]
            section[pulse, part, pl.ds(0, RADIX), :] = own
            section[pulse, part, pl.ds(RADIX, DELAY_MAX), :] = own[:DELAY_MAX]
    tables[1].wait()
    tables[2].wait()
    for pulse in range(pulse_count):
        window = pl.ds(delays[pulse], RADIX)
        real_part = section[pulse, 0, window, :]
        imag_part = section[pulse, 1, window, :]
        cosine = twiddle[0, window, :]
        sine_part = twiddle[1, window, :]
        rows = pl.ds(pulse * RADIX, RADIX)
        twisted[rows, pl.ds(0, LANES)] = (real_part * cosine - imag_part * sine_part).astype(jnp.bfloat16)
        twisted[rows, pl.ds(LANES, LANES)] = (real_part * sine_part + imag_part * cosine).astype(jnp.bfloat16)
    row_index = lax.broadcasted_iota(jnp.int32, (RADIX, LANES), 0)
    lane_index = lax.broadcasted_iota(jnp.int32, (RADIX, LANES), 1)
    gates = row_index * LANES + lane_index
    tables[3].wait()
    for pulse in range(pulse_count):
        sums = lax.dot_general(
            dft[...],
            twisted[pl.ds(pulse * RADIX, RADIX), :],
            (((1,), (1,)), ((), ())),
            preferred_element_type=jnp.float32,
        )
        inside = gates < SAMPLES - delays[pulse]
        real_part, imag_part = sums[:RADIX], sums[RADIX:]
        cosine, sine_part = near[0], near[1]
        turned[pl.ds(pulse, RADIX, stride=pulse_count), :] = jnp.where(
            inside, real_part * cosine - imag_part * sine_part, 0.0
        )
        turned[pl.ds(span + pulse, RADIX, stride=pulse_count), :] = jnp.where(
            inside, real_part * sine_part + imag_part * cosine, 0.0
        )
    block_rows = width // LANES * pulse_count
    for out, places in zip(outs, plan, strict=True):
        for index, apart in enumerate(places):
            start = pl.multiple_of((me ^ apart) * block_rows, block_rows)
            for step in range(width // LANES):
                rows = pl.ds(start + step * pulse_count, pulse_count)
                both = jnp.concatenate([turned[rows, :], turned[pl.ds(span + start + step * pulse_count, pulse_count), :]], axis=0)
                out[index, :, pl.ds(step * LANES, LANES)] = both.astype(jnp.bfloat16)


def range_compress(raw_echo, delays, depth_count, sub_pulses, plan):
    gate_count = lax.axis_size("gate")
    pulse_count = raw_echo.shape[1]
    width = SAMPLES // gate_count
    span = RADIX * pulse_count
    dft = to_bf16(real_form(dft_table()))
    twiddle, near = twiddles(), near_phases(depth_count, sub_pulses)
    return pl.pallas_call(
        functools.partial(compress_kernel, plan),
        out_shape=[
            pltpu.VMEM((len(places), 2 * pulse_count, width), jnp.bfloat16) for places in plan
        ],
        in_specs=[pl.BlockSpec(memory_space=pltpu.HBM)] * 5,
        out_specs=[pl.BlockSpec(memory_space=pltpu.VMEM)] * len(plan),
        scratch_shapes=[
            pltpu.SMEM(delays.shape, delays.dtype),
            pltpu.VMEM(raw_echo.shape, raw_echo.dtype),
            pltpu.VMEM(dft.shape, dft.dtype),
            pltpu.VMEM(twiddle.shape, twiddle.dtype),
            pltpu.VMEM(near.shape, near.dtype),
            pltpu.SemaphoreType.DMA((RAW_PIECES + 4,)),
            pltpu.VMEM((2 * span, LANES), jnp.float32),
            pltpu.VMEM((2 * RADIX, pulse_count * LANES), jnp.bfloat16),
            pltpu.VMEM((pulse_count, 2, ROWS, LANES), jnp.float32),
            pltpu.VMEM((span, 2 * LANES), jnp.bfloat16),
            pltpu.VMEM((2 * span, LANES), jnp.float32),
        ],
        compiler_params=pltpu.CompilerParams(vmem_limit_bytes=60 * 2**20),
        name="compress",
    )(delays, raw_echo, dft, twiddle, near)


def image_kernel(plan, far, has_total, table, *refs):
    arrays, refs = refs[: len(plan)], refs[len(plan) :]
    if has_total:
        total, out_far, data, columns, out, sent = refs
    else:
        out, data, columns = refs
    half = data.shape[0] // 2
    block = arrays[0].shape[1]
    me = lax.axis_index("gate")
    lower = (me ^ far) // FAR * half
    for array, (side, places) in zip(arrays, plan, strict=True):
        for index, apart in enumerate(places):
            if apart // FAR * FAR == far:
                start = side * half + (me ^ apart) * block - lower
                data[pl.ds(pl.multiple_of(start, block), block), :] = array[index]
    for side in range(2):
        source = pl.multiple_of(side * 2 * half + lower, half)
        columns[:, pl.ds(side * half, half)] = table[:, pl.ds(source, half)]
    tile = 256
    copies = []
    for row in range(0, out.shape[0], tile):
        for column in range(0, out.shape[1], tile):
            place = pl.ds(row, tile), pl.ds(column, tile)
            sums = jnp.dot(columns[place[0], :], data[:, place[1]], preferred_element_type=jnp.float32)
            if has_total:
                sums = sums + total[place]
            out[place] = sums.astype(out.dtype)
            if has_total:
                copies.append(pltpu.make_async_copy(out.at[place], out_far.at[place], sent.at[len(copies)]))
                copies[-1].start()
    for copy in copies:
        copy.wait()


def form_image(table, arrays, plan):
    rows, depth = table.shape[0], table.shape[1] // 2
    shape = rows, arrays[0].shape[-1]
    vmem = pl.BlockSpec(memory_space=pltpu.VMEM)
    total = []
    for far in (0, FAR):
        used = [i for i, (_, places) in enumerate(plan) if any(apart // FAR * FAR == far for apart in places)]
        image = pl.pallas_call(
            functools.partial(image_kernel, [plan[i] for i in used], far, bool(total)),
            out_shape=jax.ShapeDtypeStruct(shape, jnp.bfloat16) if far else pltpu.VMEM(shape, jnp.float32),
            in_specs=[vmem] * (1 + len(used) + len(total)),
            out_specs=pl.BlockSpec(memory_space=pltpu.HBM) if far else vmem,
            scratch_shapes=[pltpu.VMEM((depth, shape[1]), jnp.bfloat16), pltpu.VMEM((rows, depth), jnp.bfloat16)]
            + ([pltpu.VMEM(shape, jnp.bfloat16), pltpu.SemaphoreType.DMA((rows // 256 * (shape[1] // 256),))] if far else []),
            cost_estimate=pl.CostEstimate(
                flops=2 * depth * math.prod(shape), bytes_accessed=4 * math.prod(shape), transcendentals=0
            ),
            compiler_params=pltpu.CompilerParams(vmem_limit_bytes=32 * 2**20),
            name="image",
        )(table, *[arrays[i] for i in used], *total)
        total = [image]
    return image.reshape(2, ANGLES, shape[1])


def partner(array, axis, apart):
    return lax.ppermute(array, axis, [(i, i ^ 1 << apart) for i in range(lax.axis_size(axis))])


def merge_levels(received, pulse_count, sub_pulses, depth_count):
    half = ANGLES // 2
    sub_index = lax.axis_index("sub")
    steering = to_bf16(by_source(real_form(steer_table(sub_pulses)), pulse_count))
    current = jnp.dot(steering, received, preferred_element_type=jnp.float32).astype(jnp.bfloat16)
    current = current.reshape(2, ANGLES, -1)
    sector = jnp.zeros((), jnp.int32)
    interp = jnp.asarray(interp_table(), jnp.float32)
    for depth in range(1, depth_count + 1):
        side_bit = sub_index // 2 ** (depth - 1) % 2
        sent = lax.dynamic_slice_in_dim(current, (1 - side_bit) * half, half, axis=1)
        kept = lax.dynamic_slice_in_dim(current, side_bit * half, half, axis=1)
        arrived = partner(sent, "sub", depth - 1)
        sector = 2 * sector + side_bit
        modulus = ANGLES * 2 ** (depth + 3)
        numerator = 2 * (sector * ANGLES + jnp.arange(ANGLES, dtype=jnp.int32)) + 1 - ANGLES * 2**depth
        center = (2 * side_bit - 1) * (sub_pulses * 2 ** (depth - 1) // 2)
        total = 0.0
        for child, place in ((kept, center), (arrived, -center)):
            turns = jnp.mod(place * numerator, modulus).astype(jnp.float32) / modulus
            cosine = (jnp.cos(TWO_PI * turns) * math.sqrt(0.5))[:, None] * interp
            sine_part = (-jnp.sin(TWO_PI * turns) * math.sqrt(0.5))[:, None] * interp
            table = jnp.stack([jnp.stack([cosine, -sine_part]), jnp.stack([sine_part, cosine])])
            total = total + jnp.einsum(
                "akjh,khg->ajg", table.astype(jnp.bfloat16), child, preferred_element_type=jnp.float32
            )
        current = total.astype(jnp.bfloat16)
    return current


def swap(array, apart, other_sub=False):
    count = lax.axis_size("gate")
    if not other_sub:
        return lax.ppermute(array, "gate", [(i, i ^ apart) for i in range(count)])
    pairs = [(i, i ^ (count + apart)) for i in range(2 * count)]
    return lax.ppermute(array, ("sub", "gate"), pairs)


CORE, Y, Z, FAR = 1, 2, 4, 8


def after(array, other):
    return lax.optimization_barrier((array, other))[0]


def corner_turn(send):
    plan = [[place * Z, place * Z + Y] for place in range(4)]
    plan.append([place * Z + CORE + y for place in (0, 1, 3) for y in (0, Y)])
    plan.append([2 * Z + CORE, 2 * Z + CORE + Y])
    here, one, two, three, mates, mates_two = send(plan)
    width = here.shape[-1]
    mates = swap(mates, CORE)
    mates_two = swap(after(mates_two, mates), CORE)
    mates = mates.reshape(3, 2, -1, width)
    two = swap(two, 2 * Z)
    one = swap(jnp.stack([one, mates[1]], axis=1), Z)
    three = swap(jnp.stack([three, mates[2]], axis=1), 3 * Z)
    mates_two = swap(mates_two, 2 * Z)
    two = after(two, one)
    here = jnp.stack([here, mates[0]], axis=1)
    two = jnp.stack([two, mates_two], axis=1)
    near = [0, CORE, Z, Z + CORE]
    groups = [
        ([here[0], one[0]], [here[1], one[1]], near),
        ([two[0], three[0]], [two[1], three[1]], [FAR + i for i in near]),
    ]
    arrays, places = [], []
    for home, away, apart in groups:
        home, away = jnp.concatenate(home), jnp.concatenate(away)
        apart_y = [i + Y for i in apart]
        arrays += [home, swap(away, Y, True), swap(home, 0, True), swap(away, Y)]
        places += [(0, apart), (1, apart_y), (1, apart), (0, apart_y)]
    return arrays, places


def per_device(raw_echo, delays):
    gate_count = lax.axis_size("gate")
    sub_count = lax.axis_size("sub")
    pulse_count = raw_echo.shape[1]
    sub_pulses = pulse_count * gate_count
    depth_count = sub_count.bit_length() - 1
    send = functools.partial(range_compress, raw_echo, delays, depth_count, sub_pulses)
    if (sub_count, gate_count) != (2, 16):
        (compressed,) = send([range(gate_count)])
        me = lax.axis_index("gate")
        ordered = compressed[me ^ jnp.arange(gate_count)]
        received = lax.all_to_all(ordered, "gate", split_axis=0, concat_axis=0, tiled=True)
        received = received.reshape(2 * sub_pulses, SAMPLES // gate_count)
        return merge_levels(received, pulse_count, sub_pulses, depth_count)
    arrays, places = corner_turn(send)
    tables = jnp.asarray(image_tables(sub_pulses, pulse_count))
    table = lax.dynamic_index_in_dim(tables, lax.axis_index("sub"), 0, keepdims=False)
    return form_image(table, arrays, places)


def solution(mesh):
    placed = (P(None, ("sub", "gate"), None), P(("sub", "gate")))
    return jax.shard_map(
        per_device, mesh=mesh, in_specs=placed, out_specs=P(None, "sub", "gate"), check_vma=False
    )
```

```python
import functools
import math

import jax
import jax.numpy as jnp
import numpy as np
from jax import lax
from jax.experimental import pallas as pl
from jax.experimental.pallas import tpu as pltpu
from jax.sharding import PartitionSpec as P

RADIX = 128
SAMPLES = 16384
ANGLES = 256
DELAY_MAX = 64
LANES = 128
RAW_PIECES = 4
ROWS = RADIX + DELAY_MAX


TWO_PI = 2.0 * math.pi


def to_bf16(values):
    return np.asarray(values, np.float32).astype(jnp.bfloat16)


def rounded(values):
    return to_bf16(values).astype(np.float64)


def real_form(table):
    upper = np.concatenate([table.real, -table.imag], axis=1)
    lower = np.concatenate([table.imag, table.real], axis=1)
    return np.concatenate([upper, lower], axis=0)


def unit(phases):
    return np.cos(phases) + 1j * np.sin(phases)


def dft_table():
    counter = np.arange(RADIX)
    table = unit(-TWO_PI / RADIX * (counter[:, None] * counter[None, :] % RADIX)) / math.sqrt(RADIX)
    return rounded(table.real) + 1j * rounded(table.imag)


def twiddles():
    phases = -TWO_PI / SAMPLES * (np.arange(ROWS)[:, None] * np.arange(RADIX)[None, :])
    return np.stack([np.cos(phases), np.sin(phases)]).astype(np.float32)


def near_phases(depth_count, sub_pulses):
    centers = [sub_pulses * 2 ** (depth - 1) // 2 for depth in range(1, depth_count + 1)]
    center_sq = float(sum(center * center for center in centers))
    phases = -TWO_PI / (4 * ANGLES) * center_sq / (16.0 * (SAMPLES + np.arange(SAMPLES)))
    return np.stack([np.cos(phases), np.sin(phases)]).astype(np.float32).reshape(2, RADIX, RADIX)


def steer_table(sub_pulses):
    modulus = 16 * ANGLES
    beams = 2 * np.arange(ANGLES) - ANGLES + 1
    pulses = 2 * np.arange(sub_pulses) - sub_pulses + 1
    table = unit(-TWO_PI / modulus * (beams[:, None] * pulses[None, :] % modulus)) / math.sqrt(sub_pulses)
    return rounded(table.real) + 1j * rounded(table.imag)


def interp_table():
    distance = np.arange(ANGLES)[:, None] * 0.5 - 0.25 - np.arange(ANGLES // 2)[None, :]
    taper = np.where(np.abs(distance) < 4.0, 0.5 + 0.5 * np.cos(math.pi * distance / 4.0), 0.0)
    return rounded(np.sinc(distance) * taper)


def merge_table(depth, sector, center):
    modulus = ANGLES * 2 ** (depth + 3)
    row_index = sector * ANGLES + np.arange(ANGLES)
    numerator = 2 * row_index + 1 - ANGLES * 2**depth
    turns = (center * numerator) % modulus / modulus
    return unit(-TWO_PI * turns)[:, None] * interp_table() / math.sqrt(2.0)


def by_source(table, pulse_count):
    rows = table.shape[0]
    return table.reshape(rows, 2, -1, pulse_count).transpose(0, 2, 1, 3).reshape(rows, -1)


def image_tables(sub_pulses, pulse_count):
    half = ANGLES // 2
    steer = steer_table(sub_pulses)
    tables = []
    for sub in range(2):
        beams = steer[sub * half : (sub + 1) * half]
        own = (2 * sub - 1) * (sub_pulses // 2)
        parts = [real_form(merge_table(1, sub, center) @ beams) for center in (own, -own)]
        tables.append(np.concatenate([by_source(part, pulse_count) for part in parts], axis=1))
    return to_bf16(np.stack(tables))


def compress_kernel(
    plan, delays_far, raw_far, dft_far, twiddle_far, near_far, *refs
):
    outs = refs[: len(plan)]
    (
    delays, raw, dft, twiddle, near, arrived, lines, grid_in, section, twisted, turned,
    ) = refs[len(plan) :]
    pulse_count = raw.shape[1]
    width = outs[0].shape[-1]
    me = lax.axis_index("gate")
    span = RADIX * pulse_count
    piece = SAMPLES // RAW_PIECES
    pieces = [
        pltpu.make_async_copy(
            raw_far.at[:, :, pl.ds(index * piece, piece)],
            raw.at[:, :, pl.ds(index * piece, piece)],
            arrived.at[index],
        )
        for index in range(RAW_PIECES)
    ]
    tables = [
        pltpu.make_async_copy(far, here, arrived.at[RAW_PIECES + index])
        for index, (far, here) in enumerate(
            ((dft_far, dft), (delays_far, delays), (twiddle_far, twiddle), (near_far, near))
        )
    ]
    for copy in pieces + tables:
        copy.start()
    for step in range(RADIX):
        if step * LANES % piece == 0:
            pieces[step * LANES // piece].wait()
        for part in range(2):
            lines[pl.ds(part * span + step * pulse_count, pulse_count), :] = raw[
                part, :, pl.ds(step * LANES, LANES)
            ].astype(jnp.float32)
    for part in range(2):
        for pulse in range(pulse_count):
            grid_in[pl.ds(part * RADIX, RADIX), pl.ds(pulse * LANES, LANES)] = lines[
                pl.ds(part * span + pulse, RADIX, stride=pulse_count), :
            ].astype(jnp.bfloat16)
    tables[0].wait()
    for first in range(0, pulse_count, 4):
        columns = pl.ds(first * LANES, 4 * LANES)
        sums = jnp.dot(dft[...], grid_in[:, columns], preferred_element_type=jnp.float32)
        for pulse in range(first, first + 4):
            for part in range(2):
                own = sums[
                    part * RADIX : (part + 1) * RADIX, (pulse - first) * LANES : (pulse - first + 1) * LANES
                ]
                section[pulse, part, pl.ds(0, RADIX), :] = own
                section[pulse, part, pl.ds(RADIX, DELAY_MAX), :] = own[:DELAY_MAX]
    tables[1].wait()
    tables[2].wait()
    for pulse in range(pulse_count):
        window = pl.ds(delays[pulse], RADIX)
        real_part = section[pulse, 0, window, :]
        imag_part = section[pulse, 1, window, :]
        cosine = twiddle[0, window, :]
        sine_part = twiddle[1, window, :]
        rows = pl.ds(pulse * RADIX, RADIX)
        twisted[rows, pl.ds(0, LANES)] = (real_part * cosine - imag_part * sine_part).astype(jnp.bfloat16)
        twisted[rows, pl.ds(LANES, LANES)] = (real_part * sine_part + imag_part * cosine).astype(jnp.bfloat16)
    tables[3].wait()
    last_rows = RADIX - 8
    gates = (
        lax.broadcasted_iota(jnp.int32, (8, LANES), 0) + last_rows
    ) * LANES + lax.broadcasted_iota(jnp.int32, (8, LANES), 1)
    cosine, sine_part = near[0], near[1]
    for first in range(0, pulse_count, 4):
        sums = lax.dot_general(
            dft[...],
            twisted[pl.ds(first * RADIX, 4 * RADIX), :],
            (((1,), (1,)), ((), ())),
            preferred_element_type=jnp.float32,
        )
        for pulse in range(first, first + 4):
            own = sums[:, (pulse - first) * LANES : (pulse - first + 1) * LANES]
            real_part, imag_part = own[:RADIX], own[RADIX:]
            parts = (
                real_part * cosine - imag_part * sine_part,
                real_part * sine_part + imag_part * cosine,
            )
            inside = gates < SAMPLES - delays[pulse]
            for part, values in enumerate(parts):
                start = part * span + pulse
                turned[pl.ds(start, last_rows, stride=pulse_count), :] = values[:last_rows]
                turned[pl.ds(start + last_rows * pulse_count, 8, stride=pulse_count), :] = jnp.where(
                    inside, values[last_rows:], 0.0
                )
    block_rows = width // LANES * pulse_count
    for out, places in zip(outs, plan, strict=True):
        for index, apart in enumerate(places):
            start = pl.multiple_of((me ^ apart) * block_rows, block_rows)
            for step in range(width // LANES):
                rows = pl.ds(start + step * pulse_count, pulse_count)
                both = jnp.concatenate([turned[rows, :], turned[pl.ds(span + start + step * pulse_count, pulse_count), :]], axis=0)
                out[index, :, pl.ds(step * LANES, LANES)] = both.astype(jnp.bfloat16)


def range_compress(raw_echo, delays, depth_count, sub_pulses, plan):
    gate_count = lax.axis_size("gate")
    pulse_count = raw_echo.shape[1]
    width = SAMPLES // gate_count
    span = RADIX * pulse_count
    dft = to_bf16(real_form(dft_table()))
    twiddle, near = twiddles(), near_phases(depth_count, sub_pulses)
    return pl.pallas_call(
        functools.partial(compress_kernel, plan),
        out_shape=[
            pltpu.VMEM((len(places), 2 * pulse_count, width), jnp.bfloat16) for places in plan
        ],
        in_specs=[pl.BlockSpec(memory_space=pltpu.HBM)] * 5,
        out_specs=[pl.BlockSpec(memory_space=pltpu.VMEM)] * len(plan),
        scratch_shapes=[
            pltpu.SMEM(delays.shape, delays.dtype),
            pltpu.VMEM(raw_echo.shape, raw_echo.dtype),
            pltpu.VMEM(dft.shape, dft.dtype),
            pltpu.VMEM(twiddle.shape, twiddle.dtype),
            pltpu.VMEM(near.shape, near.dtype),
            pltpu.SemaphoreType.DMA((RAW_PIECES + 4,)),
            pltpu.VMEM((2 * span, LANES), jnp.float32),
            pltpu.VMEM((2 * RADIX, pulse_count * LANES), jnp.bfloat16),
            pltpu.VMEM((pulse_count, 2, ROWS, LANES), jnp.float32),
            pltpu.VMEM((span, 2 * LANES), jnp.bfloat16),
            pltpu.VMEM((2 * span, LANES), jnp.float32),
        ],
        compiler_params=pltpu.CompilerParams(vmem_limit_bytes=60 * 2**20),
        name="compress",
    )(delays, raw_echo, dft, twiddle, near)


def image_kernel(plan, far, has_total, table, *refs):
    arrays, refs = refs[: len(plan)], refs[len(plan) :]
    if has_total:
        total, out_far, data, columns, out, sent = refs
    else:
        out, data, columns = refs
    half = data.shape[0] // 2
    block = arrays[0].shape[1]
    me = lax.axis_index("gate")
    lower = (me ^ far) // FAR * half
    for array, (side, places) in zip(arrays, plan, strict=True):
        for index, apart in enumerate(places):
            if apart // FAR * FAR == far:
                start = side * half + (me ^ apart) * block - lower
                data[pl.ds(pl.multiple_of(start, block), block), :] = array[index]
    for side in range(2):
        source = pl.multiple_of(side * 2 * half + lower, half)
        columns[:, pl.ds(side * half, half)] = table[:, pl.ds(source, half)]
    tile = 256
    copies = []
    for row in range(0, out.shape[0], tile):
        for column in range(0, out.shape[1], tile):
            place = pl.ds(row, tile), pl.ds(column, tile)
            sums = jnp.dot(columns[place[0], :], data[:, place[1]], preferred_element_type=jnp.float32)
            if has_total:
                sums = sums + total[place]
            out[place] = sums.astype(out.dtype)
            if has_total:
                copies.append(pltpu.make_async_copy(out.at[place], out_far.at[place], sent.at[len(copies)]))
                copies[-1].start()
    for copy in copies:
        copy.wait()


def form_image(table, arrays, plan):
    rows, depth = table.shape[0], table.shape[1] // 2
    shape = rows, arrays[0].shape[-1]
    vmem = pl.BlockSpec(memory_space=pltpu.VMEM)
    total = []
    for far in (0, FAR):
        used = [i for i, (_, places) in enumerate(plan) if any(apart // FAR * FAR == far for apart in places)]
        image = pl.pallas_call(
            functools.partial(image_kernel, [plan[i] for i in used], far, bool(total)),
            out_shape=jax.ShapeDtypeStruct(shape, jnp.bfloat16) if far else pltpu.VMEM(shape, jnp.float32),
            in_specs=[vmem] * (1 + len(used) + len(total)),
            out_specs=pl.BlockSpec(memory_space=pltpu.HBM) if far else vmem,
            scratch_shapes=[pltpu.VMEM((depth, shape[1]), jnp.bfloat16), pltpu.VMEM((rows, depth), jnp.bfloat16)]
            + ([pltpu.VMEM(shape, jnp.bfloat16), pltpu.SemaphoreType.DMA((rows // 256 * (shape[1] // 256),))] if far else []),
            cost_estimate=pl.CostEstimate(
                flops=2 * depth * math.prod(shape), bytes_accessed=4 * math.prod(shape), transcendentals=0
            ),
            compiler_params=pltpu.CompilerParams(vmem_limit_bytes=32 * 2**20),
            name="image",
        )(table, *[arrays[i] for i in used], *total)
        total = [image]
    return image.reshape(2, ANGLES, shape[1])


def partner(array, axis, apart):
    return lax.ppermute(array, axis, [(i, i ^ 1 << apart) for i in range(lax.axis_size(axis))])


def merge_levels(received, pulse_count, sub_pulses, depth_count):
    half = ANGLES // 2
    sub_index = lax.axis_index("sub")
    steering = to_bf16(by_source(real_form(steer_table(sub_pulses)), pulse_count))
    current = jnp.dot(steering, received, preferred_element_type=jnp.float32).astype(jnp.bfloat16)
    current = current.reshape(2, ANGLES, -1)
    sector = jnp.zeros((), jnp.int32)
    interp = jnp.asarray(interp_table(), jnp.float32)
    for depth in range(1, depth_count + 1):
        side_bit = sub_index // 2 ** (depth - 1) % 2
        sent = lax.dynamic_slice_in_dim(current, (1 - side_bit) * half, half, axis=1)
        kept = lax.dynamic_slice_in_dim(current, side_bit * half, half, axis=1)
        arrived = partner(sent, "sub", depth - 1)
        sector = 2 * sector + side_bit
        modulus = ANGLES * 2 ** (depth + 3)
        numerator = 2 * (sector * ANGLES + jnp.arange(ANGLES, dtype=jnp.int32)) + 1 - ANGLES * 2**depth
        center = (2 * side_bit - 1) * (sub_pulses * 2 ** (depth - 1) // 2)
        total = 0.0
        for child, place in ((kept, center), (arrived, -center)):
            turns = jnp.mod(place * numerator, modulus).astype(jnp.float32) / modulus
            cosine = (jnp.cos(TWO_PI * turns) * math.sqrt(0.5))[:, None] * interp
            sine_part = (-jnp.sin(TWO_PI * turns) * math.sqrt(0.5))[:, None] * interp
            table = jnp.stack([jnp.stack([cosine, -sine_part]), jnp.stack([sine_part, cosine])])
            total = total + jnp.einsum(
                "akjh,khg->ajg", table.astype(jnp.bfloat16), child, preferred_element_type=jnp.float32
            )
        current = total.astype(jnp.bfloat16)
    return current


def swap(array, apart, other_sub=False):
    count = lax.axis_size("gate")
    if not other_sub:
        return lax.ppermute(array, "gate", [(i, i ^ apart) for i in range(count)])
    pairs = [(i, i ^ (count + apart)) for i in range(2 * count)]
    return lax.ppermute(array, ("sub", "gate"), pairs)


CORE, Y, Z, FAR = 1, 2, 4, 8


def after(array, other):
    return lax.optimization_barrier((array, other))[0]


def corner_turn(send):
    plan = [[place * Z, place * Z + Y] for place in range(4)]
    plan.append([place * Z + CORE + y for place in (0, 1, 3) for y in (0, Y)])
    plan.append([2 * Z + CORE, 2 * Z + CORE + Y])
    here, one, two, three, mates, mates_two = send(plan)
    width = here.shape[-1]
    mates = swap(mates, CORE)
    mates_two = swap(after(mates_two, mates), CORE)
    mates = mates.reshape(3, 2, -1, width)
    two = swap(two, 2 * Z)
    one = swap(jnp.stack([one, mates[1]], axis=1), Z)
    three = swap(jnp.stack([three, mates[2]], axis=1), 3 * Z)
    two_away = swap(mates_two[1:], 2 * Z)
    two_home = swap(mates_two[:1], 2 * Z)
    two = after(two, one)
    here = jnp.stack([here, mates[0]], axis=1)
    near = [0, CORE, Z, Z + CORE]
    groups = [
        ([here[0], one[0]], [here[1], one[1]], near),
        ([two[:1], two_home, three[0]], [two[1:], two_away, three[1]], [FAR + i for i in near]),
    ]
    arrays, places = [], []
    for home, away, apart in groups:
        home, away = jnp.concatenate(home), jnp.concatenate(away)
        apart_y = [i + Y for i in apart]
        arrays += [home, swap(away, Y, True), swap(home, 0, True), swap(away, Y)]
        places += [(0, apart), (1, apart_y), (1, apart), (0, apart_y)]
    return arrays, places


def per_device(raw_echo, delays):
    gate_count = lax.axis_size("gate")
    sub_count = lax.axis_size("sub")
    pulse_count = raw_echo.shape[1]
    sub_pulses = pulse_count * gate_count
    depth_count = sub_count.bit_length() - 1
    send = functools.partial(range_compress, raw_echo, delays, depth_count, sub_pulses)
    if (sub_count, gate_count) != (2, 16):
        (compressed,) = send([range(gate_count)])
        me = lax.axis_index("gate")
        ordered = compressed[me ^ jnp.arange(gate_count)]
        received = lax.all_to_all(ordered, "gate", split_axis=0, concat_axis=0, tiled=True)
        received = received.reshape(2 * sub_pulses, SAMPLES // gate_count)
        return merge_levels(received, pulse_count, sub_pulses, depth_count)
    arrays, places = corner_turn(send)
    tables = jnp.asarray(image_tables(sub_pulses, pulse_count))
    table = lax.dynamic_index_in_dim(tables, lax.axis_index("sub"), 0, keepdims=False)
    return form_image(table, arrays, places)


def solution(mesh):
    placed = (P(None, ("sub", "gate"), None), P(("sub", "gate")))
    return jax.shard_map(
        per_device, mesh=mesh, in_specs=placed, out_specs=P(None, "sub", "gate"), check_vma=False
    )
```

```python
import functools
import math

import jax
import jax.numpy as jnp
import numpy as np
from jax import lax
from jax.experimental import pallas as pl
from jax.experimental.pallas import tpu as pltpu
from jax.sharding import PartitionSpec as P

RADIX = 128
SAMPLES = 16384
ANGLES = 256
DELAY_MAX = 64
LANES = 128
RAW_PIECES = 4
ROWS = RADIX + DELAY_MAX


TWO_PI = 2.0 * math.pi


def to_bf16(values):
    return np.asarray(values, np.float32).astype(jnp.bfloat16)


def rounded(values):
    return to_bf16(values).astype(np.float64)


def real_form(table):
    upper = np.concatenate([table.real, -table.imag], axis=1)
    lower = np.concatenate([table.imag, table.real], axis=1)
    return np.concatenate([upper, lower], axis=0)


def unit(phases):
    return np.cos(phases) + 1j * np.sin(phases)


def dft_table():
    counter = np.arange(RADIX)
    table = unit(-TWO_PI / RADIX * (counter[:, None] * counter[None, :] % RADIX)) / math.sqrt(RADIX)
    return rounded(table.real) + 1j * rounded(table.imag)


def twiddles():
    phases = -TWO_PI / SAMPLES * (np.arange(ROWS)[:, None] * np.arange(RADIX)[None, :])
    return np.stack([np.cos(phases), np.sin(phases)]).astype(np.float32)


def near_phases(depth_count, sub_pulses):
    centers = [sub_pulses * 2 ** (depth - 1) // 2 for depth in range(1, depth_count + 1)]
    center_sq = float(sum(center * center for center in centers))
    phases = -TWO_PI / (4 * ANGLES) * center_sq / (16.0 * (SAMPLES + np.arange(SAMPLES)))
    return np.stack([np.cos(phases), np.sin(phases)]).astype(np.float32).reshape(2, RADIX, RADIX)


def steer_table(sub_pulses):
    modulus = 16 * ANGLES
    beams = 2 * np.arange(ANGLES) - ANGLES + 1
    pulses = 2 * np.arange(sub_pulses) - sub_pulses + 1
    table = unit(-TWO_PI / modulus * (beams[:, None] * pulses[None, :] % modulus)) / math.sqrt(sub_pulses)
    return rounded(table.real) + 1j * rounded(table.imag)


def interp_table():
    distance = np.arange(ANGLES)[:, None] * 0.5 - 0.25 - np.arange(ANGLES // 2)[None, :]
    taper = np.where(np.abs(distance) < 4.0, 0.5 + 0.5 * np.cos(math.pi * distance / 4.0), 0.0)
    return rounded(np.sinc(distance) * taper)


def merge_table(depth, sector, center):
    modulus = ANGLES * 2 ** (depth + 3)
    row_index = sector * ANGLES + np.arange(ANGLES)
    numerator = 2 * row_index + 1 - ANGLES * 2**depth
    turns = (center * numerator) % modulus / modulus
    return unit(-TWO_PI * turns)[:, None] * interp_table() / math.sqrt(2.0)


def by_source(table, pulse_count):
    rows = table.shape[0]
    return table.reshape(rows, 2, -1, pulse_count).transpose(0, 2, 1, 3).reshape(rows, -1)


def image_tables(sub_pulses, pulse_count):
    half = ANGLES // 2
    steer = steer_table(sub_pulses)
    tables = []
    for sub in range(2):
        beams = steer[sub * half : (sub + 1) * half]
        own = (2 * sub - 1) * (sub_pulses // 2)
        parts = [real_form(merge_table(1, sub, center) @ beams) for center in (own, -own)]
        tables.append(np.concatenate([by_source(part, pulse_count) for part in parts], axis=1))
    return to_bf16(np.stack(tables))


def compress_kernel(
    plan, delays_far, raw_far, dft_far, twiddle_far, near_far, *refs
):
    outs = refs[: len(plan)]
    (
    delays, raw, dft, twiddle, near, arrived, lines, grid_in, section, twisted, turned,
    ) = refs[len(plan) :]
    pulse_count = raw.shape[1]
    width = outs[0].shape[-1]
    me = lax.axis_index("gate")
    span = RADIX * pulse_count
    piece = SAMPLES // RAW_PIECES
    pieces = [
        pltpu.make_async_copy(
            raw_far.at[:, :, pl.ds(index * piece, piece)],
            raw.at[:, :, pl.ds(index * piece, piece)],
            arrived.at[index],
        )
        for index in range(RAW_PIECES)
    ]
    tables = [
        pltpu.make_async_copy(far, here, arrived.at[RAW_PIECES + index])
        for index, (far, here) in enumerate(
            ((dft_far, dft), (delays_far, delays), (twiddle_far, twiddle), (near_far, near))
        )
    ]
    for copy in pieces + tables:
        copy.start()
    for step in range(RADIX):
        if step * LANES % piece == 0:
            pieces[step * LANES // piece].wait()
        for part in range(2):
            lines[pl.ds(part * span + step * pulse_count, pulse_count), :] = raw[
                part, :, pl.ds(step * LANES, LANES)
            ].astype(jnp.float32)
    for part in range(2):
        for pulse in range(pulse_count):
            grid_in[pl.ds(part * RADIX, RADIX), pl.ds(pulse * LANES, LANES)] = lines[
                pl.ds(part * span + pulse, RADIX, stride=pulse_count), :
            ].astype(jnp.bfloat16)
    tables[0].wait()
    for first in range(0, pulse_count, 4):
        columns = pl.ds(first * LANES, 4 * LANES)
        sums = jnp.dot(dft[...], grid_in[:, columns], preferred_element_type=jnp.float32)
        for pulse in range(first, first + 4):
            for part in range(2):
                own = sums[
                    part * RADIX : (part + 1) * RADIX, (pulse - first) * LANES : (pulse - first + 1) * LANES
                ]
                section[pulse, part, pl.ds(0, RADIX), :] = own
                section[pulse, part, pl.ds(RADIX, DELAY_MAX), :] = own[:DELAY_MAX]
    tables[1].wait()
    tables[2].wait()
    for pulse in range(pulse_count):
        window = pl.ds(delays[pulse], RADIX)
        real_part = section[pulse, 0, window, :]
        imag_part = section[pulse, 1, window, :]
        cosine = twiddle[0, window, :]
        sine_part = twiddle[1, window, :]
        rows = pl.ds(pulse * RADIX, RADIX)
        twisted[rows, pl.ds(0, LANES)] = (real_part * cosine - imag_part * sine_part).astype(jnp.bfloat16)
        twisted[rows, pl.ds(LANES, LANES)] = (real_part * sine_part + imag_part * cosine).astype(jnp.bfloat16)
    tables[3].wait()
    last_rows = RADIX - 8
    gates = (
        lax.broadcasted_iota(jnp.int32, (8, LANES), 0) + last_rows
    ) * LANES + lax.broadcasted_iota(jnp.int32, (8, LANES), 1)
    cosine, sine_part = near[0], near[1]
    for first in range(0, pulse_count, 4):
        sums = lax.dot_general(
            dft[...],
            twisted[pl.ds(first * RADIX, 4 * RADIX), :],
            (((1,), (1,)), ((), ())),
            preferred_element_type=jnp.float32,
        )
        for pulse in range(first, first + 4):
            own = sums[:, (pulse - first) * LANES : (pulse - first + 1) * LANES]
            real_part, imag_part = own[:RADIX], own[RADIX:]
            parts = (
                real_part * cosine - imag_part * sine_part,
                real_part * sine_part + imag_part * cosine,
            )
            inside = gates < SAMPLES - delays[pulse]
            for part, values in enumerate(parts):
                start = part * span + pulse
                turned[pl.ds(start, last_rows, stride=pulse_count), :] = values[:last_rows]
                turned[pl.ds(start + last_rows * pulse_count, 8, stride=pulse_count), :] = jnp.where(
                    inside, values[last_rows:], 0.0
                )
    block_rows = width // LANES * pulse_count
    for out, places in zip(outs, plan, strict=True):
        for index, apart in enumerate(places):
            start = pl.multiple_of((me ^ apart) * block_rows, block_rows)
            for step in range(width // LANES):
                rows = pl.ds(start + step * pulse_count, pulse_count)
                both = jnp.concatenate([turned[rows, :], turned[pl.ds(span + start + step * pulse_count, pulse_count), :]], axis=0)
                out[index, :, pl.ds(step * LANES, LANES)] = both.astype(jnp.bfloat16)


def range_compress(raw_echo, delays, depth_count, sub_pulses, plan):
    gate_count = lax.axis_size("gate")
    pulse_count = raw_echo.shape[1]
    width = SAMPLES // gate_count
    span = RADIX * pulse_count
    dft = to_bf16(real_form(dft_table()))
    twiddle, near = twiddles(), near_phases(depth_count, sub_pulses)
    return pl.pallas_call(
        functools.partial(compress_kernel, plan),
        out_shape=[
            pltpu.VMEM((len(places), 2 * pulse_count, width), jnp.bfloat16) for places in plan
        ],
        in_specs=[pl.BlockSpec(memory_space=pltpu.HBM)] * 5,
        out_specs=[pl.BlockSpec(memory_space=pltpu.VMEM)] * len(plan),
        scratch_shapes=[
            pltpu.SMEM(delays.shape, delays.dtype),
            pltpu.VMEM(raw_echo.shape, raw_echo.dtype),
            pltpu.VMEM(dft.shape, dft.dtype),
            pltpu.VMEM(twiddle.shape, twiddle.dtype),
            pltpu.VMEM(near.shape, near.dtype),
            pltpu.SemaphoreType.DMA((RAW_PIECES + 4,)),
            pltpu.VMEM((2 * span, LANES), jnp.float32),
            pltpu.VMEM((2 * RADIX, pulse_count * LANES), jnp.bfloat16),
            pltpu.VMEM((pulse_count, 2, ROWS, LANES), jnp.float32),
            pltpu.VMEM((span, 2 * LANES), jnp.bfloat16),
            pltpu.VMEM((2 * span, LANES), jnp.float32),
        ],
        compiler_params=pltpu.CompilerParams(vmem_limit_bytes=60 * 2**20),
        name="compress",
    )(delays, raw_echo, dft, twiddle, near)


def image_kernel(plan, far, has_total, table, *refs):
    arrays, refs = refs[: len(plan)], refs[len(plan) :]
    if has_total:
        total, out_far, data, columns, out, sent = refs
    else:
        out, data, columns = refs
    half = data.shape[0] // 2
    block = arrays[0].shape[1]
    me = lax.axis_index("gate")
    lower = (me ^ far) // FAR * half
    core = me % 2
    for array, ((side, along), (side_odd, along_odd), places) in zip(arrays, plan, strict=True):
        side = side + core * (side_odd - side)
        along = along + core * (along_odd - along)
        for index, apart in enumerate(places):
            if apart // FAR * FAR == far:
                start = side * half + (me ^ (apart + along)) * block - lower
                data[pl.ds(pl.multiple_of(start, block), block), :] = array[index]
    for side in range(2):
        source = pl.multiple_of(side * 2 * half + lower, half)
        columns[:, pl.ds(side * half, half)] = table[lax.axis_index("sub"), :, pl.ds(source, half)]
    tile = 256
    copies = []
    for row in range(0, out.shape[0], tile):
        for column in range(0, out.shape[1], tile):
            place = pl.ds(row, tile), pl.ds(column, tile)
            sums = jnp.dot(columns[place[0], :], data[:, place[1]], preferred_element_type=jnp.float32)
            if has_total:
                sums = sums + total[place]
            out[place] = sums.astype(out.dtype)
            if has_total:
                copies.append(pltpu.make_async_copy(out.at[place], out_far.at[place], sent.at[len(copies)]))
                copies[-1].start()
    for copy in copies:
        copy.wait()


def form_image(tables, arrays, plan):
    rows, depth = tables.shape[1], tables.shape[2] // 2
    shape = rows, arrays[0].shape[-1]
    vmem = pl.BlockSpec(memory_space=pltpu.VMEM)
    total = []
    for far in (0, FAR):
        used = [i for i, (*_, places) in enumerate(plan) if any(apart // FAR * FAR == far for apart in places)]
        image = pl.pallas_call(
            functools.partial(image_kernel, [plan[i] for i in used], far, bool(total)),
            out_shape=jax.ShapeDtypeStruct(shape, jnp.bfloat16) if far else pltpu.VMEM(shape, jnp.float32),
            in_specs=[vmem] * (1 + len(used) + len(total)),
            out_specs=pl.BlockSpec(memory_space=pltpu.HBM) if far else vmem,
            scratch_shapes=[pltpu.VMEM((depth, shape[1]), jnp.bfloat16), pltpu.VMEM((rows, depth), jnp.bfloat16)]
            + ([pltpu.VMEM(shape, jnp.bfloat16), pltpu.SemaphoreType.DMA((rows // 256 * (shape[1] // 256),))] if far else []),
            cost_estimate=pl.CostEstimate(
                flops=2 * depth * math.prod(shape), bytes_accessed=4 * math.prod(shape), transcendentals=0
            ),
            compiler_params=pltpu.CompilerParams(vmem_limit_bytes=32 * 2**20),
            name="image",
        )(tables, *[arrays[i] for i in used], *total)
        total = [image]
    return image.reshape(2, ANGLES, shape[1])


def partner(array, axis, apart):
    return lax.ppermute(array, axis, [(i, i ^ 1 << apart) for i in range(lax.axis_size(axis))])


def merge_levels(received, pulse_count, sub_pulses, depth_count):
    half = ANGLES // 2
    sub_index = lax.axis_index("sub")
    steering = to_bf16(by_source(real_form(steer_table(sub_pulses)), pulse_count))
    current = jnp.dot(steering, received, preferred_element_type=jnp.float32).astype(jnp.bfloat16)
    current = current.reshape(2, ANGLES, -1)
    sector = jnp.zeros((), jnp.int32)
    interp = jnp.asarray(interp_table(), jnp.float32)
    for depth in range(1, depth_count + 1):
        side_bit = sub_index // 2 ** (depth - 1) % 2
        sent = lax.dynamic_slice_in_dim(current, (1 - side_bit) * half, half, axis=1)
        kept = lax.dynamic_slice_in_dim(current, side_bit * half, half, axis=1)
        arrived = partner(sent, "sub", depth - 1)
        sector = 2 * sector + side_bit
        modulus = ANGLES * 2 ** (depth + 3)
        numerator = 2 * (sector * ANGLES + jnp.arange(ANGLES, dtype=jnp.int32)) + 1 - ANGLES * 2**depth
        center = (2 * side_bit - 1) * (sub_pulses * 2 ** (depth - 1) // 2)
        total = 0.0
        for child, place in ((kept, center), (arrived, -center)):
            turns = jnp.mod(place * numerator, modulus).astype(jnp.float32) / modulus
            cosine = (jnp.cos(TWO_PI * turns) * math.sqrt(0.5))[:, None] * interp
            sine_part = (-jnp.sin(TWO_PI * turns) * math.sqrt(0.5))[:, None] * interp
            table = jnp.stack([jnp.stack([cosine, -sine_part]), jnp.stack([sine_part, cosine])])
            total = total + jnp.einsum(
                "akjh,khg->ajg", table.astype(jnp.bfloat16), child, preferred_element_type=jnp.float32
            )
        current = total.astype(jnp.bfloat16)
    return current


def swap(array, even, odd=None):
    count = 2 * lax.axis_size("gate")
    pairs = [(i, i ^ (even if odd is None or i % 2 == 0 else odd)) for i in range(count)]
    return lax.ppermute(array, ("sub", "gate"), pairs)


CORE, Y, Z, FAR = 1, 2, 4, 8


def after(array, other):
    return lax.optimization_barrier((array, other))[0]


EXCHANGES = [((1, 0), (0, Y)), ((1, Y), (1, 0)), ((0, Y), (1, Y))]


def corner_turn(send):
    plan = [[place * Z, place * Z + Y] for place in range(4)]
    plan.append([place * Z + CORE + y for place in (0, 1, 3) for y in (0, Y)])
    plan.append([2 * Z + CORE, 2 * Z + CORE + Y])
    here, one, two, three, mates, mates_two = send(plan)
    width = here.shape[-1]
    mates = swap(mates, CORE)
    mates_two = swap(after(mates_two, mates), CORE)
    mates = mates.reshape(3, 2, -1, width)
    two = swap(two, 2 * Z)
    one = swap(jnp.stack([one, mates[1]], axis=1), Z)
    three = swap(jnp.stack([three, mates[2]], axis=1), 3 * Z)
    mates_two = swap(mates_two, 2 * Z)
    two = after(two, one)
    here = jnp.stack([here, mates[0]], axis=1)
    groups = [
        ([here[0], one[0], two[:1]], [here[1], one[1], two[1:]], [0, CORE, Z, Z + CORE, FAR]),
        ([mates_two[:1], three[0]], [mates_two[1:], three[1]], [FAR + CORE, FAR + Z, FAR + Z + CORE]),
    ]
    first_core = lax.axis_index("gate") % 2 == 0
    across = lax.axis_size("gate")
    arrays, places = [], []
    for home, away, apart in groups:
        home, away = jnp.concatenate(home), jnp.concatenate(away)
        arrays.append(home)
        places.append(((0, 0), (0, 0), apart))
        for even, odd in EXCHANGES:
            blocks = [away if along else home for _, along in (even, odd)]
            sent = away if even[1] and odd[1] else jnp.where(first_core, *blocks)
            arrays.append(swap(sent, *(side * across + along for side, along in (even, odd))))
            places.append((even, odd, apart))
    return arrays, places


def per_device(raw_echo, delays):
    gate_count = lax.axis_size("gate")
    sub_count = lax.axis_size("sub")
    pulse_count = raw_echo.shape[1]
    sub_pulses = pulse_count * gate_count
    depth_count = sub_count.bit_length() - 1
    send = functools.partial(range_compress, raw_echo, delays, depth_count, sub_pulses)
    if (sub_count, gate_count) != (2, 16):
        (compressed,) = send([range(gate_count)])
        me = lax.axis_index("gate")
        ordered = compressed[me ^ jnp.arange(gate_count)]
        received = lax.all_to_all(ordered, "gate", split_axis=0, concat_axis=0, tiled=True)
        received = received.reshape(2 * sub_pulses, SAMPLES // gate_count)
        return merge_levels(received, pulse_count, sub_pulses, depth_count)
    arrays, places = corner_turn(send)
    return form_image(image_tables(sub_pulses, pulse_count), arrays, places)


def solution(mesh):
    placed = (P(None, ("sub", "gate"), None), P(("sub", "gate")))
    return jax.shard_map(
        per_device, mesh=mesh, in_specs=placed, out_specs=P(None, "sub", "gate"), check_vma=False
    )
```

```python
import functools
import math

import jax
import jax.numpy as jnp
import numpy as np
from jax import lax
from jax.experimental import pallas as pl
from jax.experimental.pallas import tpu as pltpu
from jax.sharding import PartitionSpec as P

RADIX = 128
SAMPLES = 16384
ANGLES = 256
DELAY_MAX = 64
LANES = 128
RAW_PIECES = 4
ROWS = RADIX + DELAY_MAX + 8


TWO_PI = 2.0 * math.pi


def to_bf16(values):
    return np.asarray(values, np.float32).astype(jnp.bfloat16)


def rounded(values):
    return to_bf16(values).astype(np.float64)


def real_form(table):
    upper = np.concatenate([table.real, -table.imag], axis=1)
    lower = np.concatenate([table.imag, table.real], axis=1)
    return np.concatenate([upper, lower], axis=0)


def unit(phases):
    return np.cos(phases) + 1j * np.sin(phases)


def dft_table():
    counter = np.arange(RADIX)
    table = unit(-TWO_PI / RADIX * (counter[:, None] * counter[None, :] % RADIX)) / math.sqrt(RADIX)
    return rounded(table.real) + 1j * rounded(table.imag)


def twiddles():
    phases = -TWO_PI / SAMPLES * (np.arange(ROWS)[:, None] * np.arange(RADIX)[None, :])
    return np.stack([np.cos(phases), np.sin(phases)]).astype(np.float32)


def near_phases(depth_count, sub_pulses):
    centers = [sub_pulses * 2 ** (depth - 1) // 2 for depth in range(1, depth_count + 1)]
    center_sq = float(sum(center * center for center in centers))
    phases = -TWO_PI / (4 * ANGLES) * center_sq / (16.0 * (SAMPLES + np.arange(SAMPLES)))
    return np.stack([np.cos(phases), np.sin(phases)]).astype(np.float32).reshape(2, RADIX, RADIX)


def steer_table(sub_pulses):
    modulus = 16 * ANGLES
    beams = 2 * np.arange(ANGLES) - ANGLES + 1
    pulses = 2 * np.arange(sub_pulses) - sub_pulses + 1
    table = unit(-TWO_PI / modulus * (beams[:, None] * pulses[None, :] % modulus)) / math.sqrt(sub_pulses)
    return rounded(table.real) + 1j * rounded(table.imag)


def interp_table():
    distance = np.arange(ANGLES)[:, None] * 0.5 - 0.25 - np.arange(ANGLES // 2)[None, :]
    taper = np.where(np.abs(distance) < 4.0, 0.5 + 0.5 * np.cos(math.pi * distance / 4.0), 0.0)
    return rounded(np.sinc(distance) * taper)


def merge_table(depth, sector, center):
    modulus = ANGLES * 2 ** (depth + 3)
    row_index = sector * ANGLES + np.arange(ANGLES)
    numerator = 2 * row_index + 1 - ANGLES * 2**depth
    turns = (center * numerator) % modulus / modulus
    return unit(-TWO_PI * turns)[:, None] * interp_table() / math.sqrt(2.0)


def by_source(table, pulse_count):
    rows = table.shape[0]
    return table.reshape(rows, 2, -1, pulse_count).transpose(0, 2, 1, 3).reshape(rows, -1)


def image_tables(sub_pulses, pulse_count):
    half = ANGLES // 2
    steer = steer_table(sub_pulses)
    tables = []
    for sub in range(2):
        beams = steer[sub * half : (sub + 1) * half]
        own = (2 * sub - 1) * (sub_pulses // 2)
        parts = [real_form(merge_table(1, sub, center) @ beams) for center in (own, -own)]
        tables.append(np.concatenate([by_source(part, pulse_count) for part in parts], axis=1))
    return to_bf16(np.stack(tables))


def compress_kernel(plan, delays_far, raw_far, dft_far, twiddle_far, near_far, *refs):
    outs, scratch = refs[: len(plan)], refs[len(plan) :]
    delays, raw, dft, twiddle, near, arrived, lines, grid_in, section, twisted, turned = scratch
    pulse_count = raw.shape[1]
    width = outs[0].shape[-1]
    me = lax.axis_index("gate")
    span = RADIX * pulse_count
    piece = SAMPLES // RAW_PIECES
    pieces = [
        pltpu.make_async_copy(
            raw_far.at[:, :, pl.ds(index * piece, piece)],
            raw.at[:, :, pl.ds(index * piece, piece)],
            arrived.at[index],
        )
        for index in range(RAW_PIECES)
    ]
    tables = [
        pltpu.make_async_copy(far, here, arrived.at[RAW_PIECES + index])
        for index, (far, here) in enumerate(
            ((dft_far, dft), (delays_far, delays), (twiddle_far, twiddle), (near_far, near))
        )
    ]
    for copy in pieces + tables:
        copy.start()
    for step in range(RADIX):
        if step * LANES % piece == 0:
            pieces[step * LANES // piece].wait()
        for part in range(2):
            lines[pl.ds(part * span + step * pulse_count, pulse_count), :] = raw[
                part, :, pl.ds(step * LANES, LANES)
            ].astype(jnp.float32)
    for part in range(2):
        for pulse in range(pulse_count):
            grid_in[pl.ds(part * RADIX, RADIX), pl.ds(pulse * LANES, LANES)] = lines[
                pl.ds(part * span + pulse, RADIX, stride=pulse_count), :
            ].astype(jnp.bfloat16)
    tables[0].wait()
    for first in range(0, pulse_count, 4):
        columns = pl.ds(first * LANES, 4 * LANES)
        sums = jnp.dot(dft[...], grid_in[:, columns], preferred_element_type=jnp.float32)
        for pulse in range(first, first + 4):
            for part in range(2):
                own = sums[
                    part * RADIX : (part + 1) * RADIX, (pulse - first) * LANES : (pulse - first + 1) * LANES
                ]
                section[pulse, part, pl.ds(0, RADIX), :] = own
                section[pulse, part, pl.ds(RADIX, DELAY_MAX), :] = own[:DELAY_MAX]
    tables[1].wait()
    tables[2].wait()
    for pulse in range(pulse_count):
        window = pl.ds(delays[pulse], RADIX)
        real_part = section[pulse, 0, window, :]
        imag_part = section[pulse, 1, window, :]
        cosine = twiddle[0, window, :]
        sine_part = twiddle[1, window, :]
        rows = pl.ds(pulse * RADIX, RADIX)
        twisted[rows, pl.ds(0, LANES)] = (real_part * cosine - imag_part * sine_part).astype(jnp.bfloat16)
        twisted[rows, pl.ds(LANES, LANES)] = (real_part * sine_part + imag_part * cosine).astype(jnp.bfloat16)
    tables[3].wait()
    last_rows = RADIX - 8
    gates = (
        lax.broadcasted_iota(jnp.int32, (8, LANES), 0) + last_rows
    ) * LANES + lax.broadcasted_iota(jnp.int32, (8, LANES), 1)
    cosine, sine_part = near[0], near[1]
    for first in range(0, pulse_count, 4):
        sums = lax.dot_general(
            dft[...],
            twisted[pl.ds(first * RADIX, 4 * RADIX), :],
            (((1,), (1,)), ((), ())),
            preferred_element_type=jnp.float32,
        )
        for pulse in range(first, first + 4):
            own = sums[:, (pulse - first) * LANES : (pulse - first + 1) * LANES]
            real_part, imag_part = own[:RADIX], own[RADIX:]
            parts = (
                real_part * cosine - imag_part * sine_part,
                real_part * sine_part + imag_part * cosine,
            )
            inside = gates < SAMPLES - delays[pulse]
            for part, values in enumerate(parts):
                start = part * span + pulse
                turned[pl.ds(start, last_rows, stride=pulse_count), :] = values[:last_rows]
                turned[pl.ds(start + last_rows * pulse_count, 8, stride=pulse_count), :] = jnp.where(
                    inside, values[last_rows:], 0.0
                )
    block_rows = width // LANES * pulse_count
    for out, places in zip(outs, plan, strict=True):
        for index, apart in enumerate(places):
            start = pl.multiple_of((me ^ apart) * block_rows, block_rows)
            for step in range(width // LANES):
                rows = pl.ds(start + step * pulse_count, pulse_count)
                imag_rows = pl.ds(span + start + step * pulse_count, pulse_count)
                both = jnp.concatenate([turned[rows, :], turned[imag_rows, :]], axis=0)
                out[index, :, pl.ds(step * LANES, LANES)] = both.astype(jnp.bfloat16)


def range_compress(raw_echo, delays, depth_count, sub_pulses, plan):
    gate_count = lax.axis_size("gate")
    pulse_count = raw_echo.shape[1]
    width = SAMPLES // gate_count
    span = RADIX * pulse_count
    dft = to_bf16(real_form(dft_table()))
    twiddle, near = twiddles(), near_phases(depth_count, sub_pulses)
    return pl.pallas_call(
        functools.partial(compress_kernel, plan),
        out_shape=[
            pltpu.VMEM((len(places), 2 * pulse_count, width), jnp.bfloat16) for places in plan
        ],
        in_specs=[pl.BlockSpec(memory_space=pltpu.HBM)] * 5,
        out_specs=[pl.BlockSpec(memory_space=pltpu.VMEM)] * len(plan),
        scratch_shapes=[
            pltpu.SMEM(delays.shape, delays.dtype),
            pltpu.VMEM(raw_echo.shape, raw_echo.dtype),
            pltpu.VMEM(dft.shape, dft.dtype),
            pltpu.VMEM(twiddle.shape, twiddle.dtype),
            pltpu.VMEM(near.shape, near.dtype),
            pltpu.SemaphoreType.DMA((RAW_PIECES + 4,)),
            pltpu.VMEM((2 * span + pulse_count, LANES), jnp.float32),
            pltpu.VMEM((2 * RADIX, pulse_count * LANES), jnp.bfloat16),
            pltpu.VMEM((pulse_count, 2, ROWS, LANES), jnp.float32),
            pltpu.VMEM((span, 2 * LANES), jnp.bfloat16),
            pltpu.VMEM((2 * span + pulse_count, LANES), jnp.float32),
        ],
        compiler_params=pltpu.CompilerParams(vmem_limit_bytes=60 * 2**20),
        name="compress",
    )(delays, raw_echo, dft, twiddle, near)


def image_kernel(plan, far, has_total, table, *refs):
    arrays, refs = refs[: len(plan)], refs[len(plan) :]
    if has_total:
        total, out_far, data, columns, out, sent = refs
    else:
        out, data, columns = refs
    half = data.shape[0] // 2
    block = arrays[0].shape[1]
    me = lax.axis_index("gate")
    lower = (me ^ far) // FAR * half
    core = me % 2
    for array, ((side, along), (side_odd, along_odd), places) in zip(arrays, plan, strict=True):
        side = side + core * (side_odd - side)
        along = along + core * (along_odd - along)
        for index, apart in enumerate(places):
            if apart // FAR * FAR == far:
                start = side * half + (me ^ (apart + along)) * block - lower
                data[pl.ds(pl.multiple_of(start, block), block), :] = array[index]
    for side in range(2):
        source = pl.multiple_of(side * 2 * half + lower, half)
        columns[:, pl.ds(side * half, half)] = table[lax.axis_index("sub"), :, pl.ds(source, half)]
    tile = 256
    copies = []
    for row in range(0, out.shape[0], tile):
        for column in range(0, out.shape[1], tile):
            place = pl.ds(row, tile), pl.ds(column, tile)
            sums = jnp.dot(columns[place[0], :], data[:, place[1]], preferred_element_type=jnp.float32)
            if has_total:
                sums = sums + total[place]
            out[place] = sums.astype(out.dtype)
            if has_total:
                copies.append(pltpu.make_async_copy(out.at[place], out_far.at[place], sent.at[len(copies)]))
                copies[-1].start()
    for copy in copies:
        copy.wait()


def form_image(tables, arrays, plan):
    rows, depth = tables.shape[1], tables.shape[2] // 2
    shape = rows, arrays[0].shape[-1]
    vmem = pl.BlockSpec(memory_space=pltpu.VMEM)
    total = []
    for far in (0, FAR):
        used = [i for i, (*_, places) in enumerate(plan) if any(apart // FAR * FAR == far for apart in places)]
        image = pl.pallas_call(
            functools.partial(image_kernel, [plan[i] for i in used], far, bool(total)),
            out_shape=jax.ShapeDtypeStruct(shape, jnp.bfloat16) if far else pltpu.VMEM(shape, jnp.float32),
            in_specs=[vmem] * (1 + len(used) + len(total)),
            out_specs=pl.BlockSpec(memory_space=pltpu.HBM) if far else vmem,
            scratch_shapes=[pltpu.VMEM((depth, shape[1]), jnp.bfloat16), pltpu.VMEM((rows, depth), jnp.bfloat16)]
            + ([pltpu.VMEM(shape, jnp.bfloat16), pltpu.SemaphoreType.DMA((rows // 256 * (shape[1] // 256),))] if far else []),
            cost_estimate=pl.CostEstimate(
                flops=2 * depth * math.prod(shape), bytes_accessed=4 * math.prod(shape), transcendentals=0
            ),
            compiler_params=pltpu.CompilerParams(vmem_limit_bytes=32 * 2**20),
            name="image",
        )(tables, *[arrays[i] for i in used], *total)
        total = [image]
    return image.reshape(2, ANGLES, shape[1])


def partner(array, axis, apart):
    return lax.ppermute(array, axis, [(i, i ^ 1 << apart) for i in range(lax.axis_size(axis))])


def merge_levels(received, pulse_count, sub_pulses, depth_count):
    half = ANGLES // 2
    sub_index = lax.axis_index("sub")
    steering = to_bf16(by_source(real_form(steer_table(sub_pulses)), pulse_count))
    current = jnp.dot(steering, received, preferred_element_type=jnp.float32).astype(jnp.bfloat16)
    current = current.reshape(2, ANGLES, -1)
    sector = jnp.zeros((), jnp.int32)
    interp = jnp.asarray(interp_table(), jnp.float32)
    for depth in range(1, depth_count + 1):
        side_bit = sub_index // 2 ** (depth - 1) % 2
        sent = lax.dynamic_slice_in_dim(current, (1 - side_bit) * half, half, axis=1)
        kept = lax.dynamic_slice_in_dim(current, side_bit * half, half, axis=1)
        arrived = partner(sent, "sub", depth - 1)
        sector = 2 * sector + side_bit
        modulus = ANGLES * 2 ** (depth + 3)
        numerator = 2 * (sector * ANGLES + jnp.arange(ANGLES, dtype=jnp.int32)) + 1 - ANGLES * 2**depth
        center = (2 * side_bit - 1) * (sub_pulses * 2 ** (depth - 1) // 2)
        total = 0.0
        for child, place in ((kept, center), (arrived, -center)):
            turns = jnp.mod(place * numerator, modulus).astype(jnp.float32) / modulus
            cosine = (jnp.cos(TWO_PI * turns) * math.sqrt(0.5))[:, None] * interp
            sine_part = (-jnp.sin(TWO_PI * turns) * math.sqrt(0.5))[:, None] * interp
            table = jnp.stack([jnp.stack([cosine, -sine_part]), jnp.stack([sine_part, cosine])])
            total = total + jnp.einsum(
                "akjh,khg->ajg", table.astype(jnp.bfloat16), child, preferred_element_type=jnp.float32
            )
        current = total.astype(jnp.bfloat16)
    return current


def swap(array, even, odd=None):
    count = 2 * lax.axis_size("gate")
    pairs = [(i, i ^ (even if odd is None or i % 2 == 0 else odd)) for i in range(count)]
    return lax.ppermute(array, ("sub", "gate"), pairs)


CORE, Y, Z, FAR = 1, 2, 4, 8


def after(array, other):
    return lax.optimization_barrier((array, other))[0]


EXCHANGES = [((1, 0), (0, Y)), ((1, Y), (1, 0)), ((0, Y), (1, Y))]


def corner_turn(send):
    plan = [[place * Z, place * Z + Y] for place in range(4)]
    plan.append([place * Z + CORE + y for place in (0, 1, 3) for y in (0, Y)])
    plan.append([2 * Z + CORE, 2 * Z + CORE + Y])
    here, one, two, three, mates, mates_two = send(plan)
    width = here.shape[-1]
    mates = swap(mates, CORE)
    mates_two = swap(after(mates_two, mates), CORE)
    mates = mates.reshape(3, 2, -1, width)
    two = swap(two, 2 * Z)
    one = swap(jnp.stack([one, mates[1]], axis=1), Z)
    three = swap(jnp.stack([three, mates[2]], axis=1), 3 * Z)
    mates_two = swap(mates_two, 2 * Z)
    two = after(two, one)
    here = jnp.stack([here, mates[0]], axis=1)
    groups = [
        ([here[0], one[0], two[:1]], [here[1], one[1], two[1:]], [0, CORE, Z, Z + CORE, FAR]),
        ([mates_two[:1], three[0]], [mates_two[1:], three[1]], [FAR + CORE, FAR + Z, FAR + Z + CORE]),
    ]
    first_core = lax.axis_index("gate") % 2 == 0
    across = lax.axis_size("gate")
    arrays, places = [], []
    for home, away, apart in groups:
        home, away = jnp.concatenate(home), jnp.concatenate(away)
        arrays.append(home)
        places.append(((0, 0), (0, 0), apart))
        for even, odd in EXCHANGES:
            blocks = [away if along else home for _, along in (even, odd)]
            sent = away if even[1] and odd[1] else jnp.where(first_core, *blocks)
            arrays.append(swap(sent, *(side * across + along for side, along in (even, odd))))
            places.append((even, odd, apart))
    return arrays, places


def per_device(raw_echo, delays):
    gate_count = lax.axis_size("gate")
    sub_count = lax.axis_size("sub")
    pulse_count = raw_echo.shape[1]
    sub_pulses = pulse_count * gate_count
    depth_count = sub_count.bit_length() - 1
    send = functools.partial(range_compress, raw_echo, delays, depth_count, sub_pulses)
    if (sub_count, gate_count) != (2, 16):
        (compressed,) = send([range(gate_count)])
        me = lax.axis_index("gate")
        ordered = compressed[me ^ jnp.arange(gate_count)]
        received = lax.all_to_all(ordered, "gate", split_axis=0, concat_axis=0, tiled=True)
        received = received.reshape(2 * sub_pulses, SAMPLES // gate_count)
        return merge_levels(received, pulse_count, sub_pulses, depth_count)
    arrays, places = corner_turn(send)
    return form_image(image_tables(sub_pulses, pulse_count), arrays, places)


def solution(mesh):
    placed = (P(None, ("sub", "gate"), None), P(("sub", "gate")))
    return jax.shard_map(
        per_device, mesh=mesh, in_specs=placed, out_specs=P(None, "sub", "gate"), check_vma=False
    )
```

```python
import functools
import math

import jax
import jax.numpy as jnp
import numpy as np
from jax import lax
from jax.experimental import pallas as pl
from jax.experimental.pallas import tpu as pltpu
from jax.sharding import PartitionSpec as P

RADIX = 128
SAMPLES = 16384
ANGLES = 256
DELAY_MAX = 64
LANES = 128
RAW_PIECES = 4
ROWS = RADIX + DELAY_MAX


TWO_PI = 2.0 * math.pi


def to_bf16(values):
    return np.asarray(values, np.float32).astype(jnp.bfloat16)


def rounded(values):
    return to_bf16(values).astype(np.float64)


def real_form(table):
    upper = np.concatenate([table.real, -table.imag], axis=1)
    lower = np.concatenate([table.imag, table.real], axis=1)
    return np.concatenate([upper, lower], axis=0)


def unit(phases):
    return np.cos(phases) + 1j * np.sin(phases)


def dft_table():
    counter = np.arange(RADIX)
    table = unit(-TWO_PI / RADIX * (counter[:, None] * counter[None, :] % RADIX)) / math.sqrt(RADIX)
    return rounded(table.real) + 1j * rounded(table.imag)


def twiddles():
    phases = -TWO_PI / SAMPLES * (np.arange(ROWS)[:, None] * np.arange(RADIX)[None, :])
    return np.stack([np.cos(phases), np.sin(phases)]).astype(np.float32)


def near_phases(depth_count, sub_pulses):
    centers = [sub_pulses * 2 ** (depth - 1) // 2 for depth in range(1, depth_count + 1)]
    center_sq = float(sum(center * center for center in centers))
    phases = -TWO_PI / (4 * ANGLES) * center_sq / (16.0 * (SAMPLES + np.arange(SAMPLES)))
    return np.stack([np.cos(phases), np.sin(phases)]).astype(np.float32).reshape(2, RADIX, RADIX)


def steer_table(sub_pulses):
    modulus = 16 * ANGLES
    beams = 2 * np.arange(ANGLES) - ANGLES + 1
    pulses = 2 * np.arange(sub_pulses) - sub_pulses + 1
    table = unit(-TWO_PI / modulus * (beams[:, None] * pulses[None, :] % modulus)) / math.sqrt(sub_pulses)
    return rounded(table.real) + 1j * rounded(table.imag)


def interp_table():
    distance = np.arange(ANGLES)[:, None] * 0.5 - 0.25 - np.arange(ANGLES // 2)[None, :]
    taper = np.where(np.abs(distance) < 4.0, 0.5 + 0.5 * np.cos(math.pi * distance / 4.0), 0.0)
    return rounded(np.sinc(distance) * taper)


def merge_table(depth, sector, center):
    modulus = ANGLES * 2 ** (depth + 3)
    row_index = sector * ANGLES + np.arange(ANGLES)
    numerator = 2 * row_index + 1 - ANGLES * 2**depth
    turns = (center * numerator) % modulus / modulus
    return unit(-TWO_PI * turns)[:, None] * interp_table() / math.sqrt(2.0)


def by_source(table, pulse_count):
    rows = table.shape[0]
    return table.reshape(rows, 2, -1, pulse_count).transpose(0, 2, 1, 3).reshape(rows, -1)


def image_tables(sub_pulses, pulse_count):
    half = ANGLES // 2
    steer = steer_table(sub_pulses)
    tables = []
    for sub in range(2):
        beams = steer[sub * half : (sub + 1) * half]
        own = (2 * sub - 1) * (sub_pulses // 2)
        parts = [real_form(merge_table(1, sub, center) @ beams) for center in (own, -own)]
        tables.append(np.concatenate([by_source(part, pulse_count) for part in parts], axis=1))
    return to_bf16(np.stack(tables))


def compress_kernel(plan, delays_far, raw_far, dft_far, twiddle_far, near_far, *refs):
    outs, scratch = refs[: len(plan)], refs[len(plan) :]
    delays, raw, dft, twiddle, near, arrived, lines, grid_in, section, twisted, turned = scratch
    pulse_count = raw.shape[1]
    width = outs[0].shape[-1]
    me = lax.axis_index("gate")
    span = RADIX * pulse_count
    piece = SAMPLES // RAW_PIECES
    pieces = [
        pltpu.make_async_copy(
            raw_far.at[:, :, pl.ds(index * piece, piece)],
            raw.at[:, :, pl.ds(index * piece, piece)],
            arrived.at[index],
        )
        for index in range(RAW_PIECES)
    ]
    tables = [
        pltpu.make_async_copy(far, here, arrived.at[RAW_PIECES + index])
        for index, (far, here) in enumerate(
            ((dft_far, dft), (delays_far, delays), (twiddle_far, twiddle), (near_far, near))
        )
    ]
    for copy in pieces + tables:
        copy.start()
    for step in range(RADIX):
        if step * LANES % piece == 0:
            pieces[step * LANES // piece].wait()
        for part in range(2):
            lines[pl.ds(part * span + step * pulse_count, pulse_count), :] = raw[
                part, :, pl.ds(step * LANES, LANES)
            ].astype(jnp.float32)
    for part in range(2):
        for pulse in range(pulse_count):
            grid_in[pl.ds(part * RADIX, RADIX), pl.ds(pulse * LANES, LANES)] = lines[
                pl.ds(part * span + pulse, RADIX, stride=pulse_count), :
            ].astype(jnp.bfloat16)
    tables[0].wait()
    for first in range(0, pulse_count, 4):
        columns = pl.ds(first * LANES, 4 * LANES)
        sums = jnp.dot(dft[...], grid_in[:, columns], preferred_element_type=jnp.float32)
        for pulse in range(first, first + 4):
            for part in range(2):
                own = sums[
                    part * RADIX : (part + 1) * RADIX, (pulse - first) * LANES : (pulse - first + 1) * LANES
                ]
                section[pulse, part, pl.ds(0, RADIX), :] = own
                section[pulse, part, pl.ds(RADIX, DELAY_MAX), :] = own[:DELAY_MAX]
    tables[1].wait()
    tables[2].wait()
    for pulse in range(pulse_count):
        window = pl.ds(delays[pulse], RADIX)
        real_part = section[pulse, 0, window, :]
        imag_part = section[pulse, 1, window, :]
        cosine = twiddle[0, window, :]
        sine_part = twiddle[1, window, :]
        rows = pl.ds(pulse * RADIX, RADIX)
        twisted[rows, pl.ds(0, LANES)] = (real_part * cosine - imag_part * sine_part).astype(jnp.bfloat16)
        twisted[rows, pl.ds(LANES, LANES)] = (real_part * sine_part + imag_part * cosine).astype(jnp.bfloat16)
    tables[3].wait()
    last_rows = RADIX - 8
    gates = (
        lax.broadcasted_iota(jnp.int32, (8, LANES), 0) + last_rows
    ) * LANES + lax.broadcasted_iota(jnp.int32, (8, LANES), 1)
    cosine, sine_part = near[0], near[1]
    for first in range(0, pulse_count, 4):
        sums = lax.dot_general(
            dft[...],
            twisted[pl.ds(first * RADIX, 4 * RADIX), :],
            (((1,), (1,)), ((), ())),
            preferred_element_type=jnp.float32,
        )
        for pulse in range(first, first + 4):
            own = sums[:, (pulse - first) * LANES : (pulse - first + 1) * LANES]
            real_part, imag_part = own[:RADIX], own[RADIX:]
            parts = (
                real_part * cosine - imag_part * sine_part,
                real_part * sine_part + imag_part * cosine,
            )
            inside = gates < SAMPLES - delays[pulse]
            for part, values in enumerate(parts):
                start = part * span + pulse
                turned[pl.ds(start, last_rows, stride=pulse_count), :] = values[:last_rows]
                turned[pl.ds(start + last_rows * pulse_count, 8, stride=pulse_count), :] = jnp.where(
                    inside, values[last_rows:], 0.0
                )
    block_rows = width // LANES * pulse_count
    for out, places in zip(outs, plan, strict=True):
        for index, apart in enumerate(places):
            start = pl.multiple_of((me ^ apart) * block_rows, block_rows)
            for step in range(width // LANES):
                rows = pl.ds(start + step * pulse_count, pulse_count)
                imag_rows = pl.ds(span + start + step * pulse_count, pulse_count)
                both = jnp.concatenate([turned[rows, :], turned[imag_rows, :]], axis=0)
                out[index, :, pl.ds(step * LANES, LANES)] = both.astype(jnp.bfloat16)


def range_compress(raw_echo, delays, depth_count, sub_pulses, plan):
    gate_count = lax.axis_size("gate")
    pulse_count = raw_echo.shape[1]
    width = SAMPLES // gate_count
    span = RADIX * pulse_count
    dft = to_bf16(real_form(dft_table()))
    twiddle, near = twiddles(), near_phases(depth_count, sub_pulses)
    return pl.pallas_call(
        functools.partial(compress_kernel, plan),
        out_shape=[
            pltpu.VMEM((len(places), 2 * pulse_count, width), jnp.bfloat16) for places in plan
        ],
        in_specs=[pl.BlockSpec(memory_space=pltpu.HBM)] * 5,
        out_specs=[pl.BlockSpec(memory_space=pltpu.VMEM)] * len(plan),
        scratch_shapes=[
            pltpu.SMEM(delays.shape, delays.dtype),
            pltpu.VMEM(raw_echo.shape, raw_echo.dtype),
            pltpu.VMEM(dft.shape, dft.dtype),
            pltpu.VMEM(twiddle.shape, twiddle.dtype),
            pltpu.VMEM(near.shape, near.dtype),
            pltpu.SemaphoreType.DMA((RAW_PIECES + 4,)),
            pltpu.VMEM((2 * span + pulse_count, LANES), jnp.float32),
            pltpu.VMEM((2 * RADIX, pulse_count * LANES), jnp.bfloat16),
            pltpu.VMEM((pulse_count, 2, ROWS, LANES), jnp.float32),
            pltpu.VMEM((span, 2 * LANES), jnp.bfloat16),
            pltpu.VMEM((2 * span + pulse_count, LANES), jnp.float32),
        ],
        compiler_params=pltpu.CompilerParams(vmem_limit_bytes=60 * 2**20),
        name="compress",
    )(delays, raw_echo, dft, twiddle, near)


def image_kernel(plan, far, has_total, table, *refs):
    arrays, refs = refs[: len(plan)], refs[len(plan) :]
    if has_total:
        total, out_far, data, columns, out, sent = refs
    else:
        out, data, columns = refs
    half = data.shape[0] // 2
    block = arrays[0].shape[1]
    me = lax.axis_index("gate")
    lower = (me ^ far) // FAR * half
    core = me % 2
    for array, ((side, along), (side_odd, along_odd), places) in zip(arrays, plan, strict=True):
        side = side + core * (side_odd - side)
        along = along + core * (along_odd - along)
        for index, apart in enumerate(places):
            if apart // FAR * FAR == far:
                start = side * half + (me ^ (apart + along)) * block - lower
                data[pl.ds(pl.multiple_of(start, block), block), :] = array[index]
    for side in range(2):
        source = pl.multiple_of(side * 2 * half + lower, half)
        columns[:, pl.ds(side * half, half)] = table[lax.axis_index("sub"), :, pl.ds(source, half)]
    tile = 256
    copies = []
    for row in range(0, out.shape[0], tile):
        for column in range(0, out.shape[1], tile):
            place = pl.ds(row, tile), pl.ds(column, tile)
            sums = jnp.dot(columns[place[0], :], data[:, place[1]], preferred_element_type=jnp.float32)
            if has_total:
                sums = sums + total[place]
            out[place] = sums.astype(out.dtype)
            if has_total:
                copies.append(pltpu.make_async_copy(out.at[place], out_far.at[place], sent.at[len(copies)]))
                copies[-1].start()
    for copy in copies:
        copy.wait()


def form_image(tables, arrays, plan):
    rows, depth = tables.shape[1], tables.shape[2] // 2
    shape = rows, arrays[0].shape[-1]
    vmem = pl.BlockSpec(memory_space=pltpu.VMEM)
    total = []
    for far in (0, FAR):
        used = [i for i, (*_, places) in enumerate(plan) if any(apart // FAR * FAR == far for apart in places)]
        image = pl.pallas_call(
            functools.partial(image_kernel, [plan[i] for i in used], far, bool(total)),
            out_shape=jax.ShapeDtypeStruct(shape, jnp.bfloat16) if far else pltpu.VMEM(shape, jnp.float32),
            in_specs=[vmem] * (1 + len(used) + len(total)),
            out_specs=pl.BlockSpec(memory_space=pltpu.HBM) if far else vmem,
            scratch_shapes=[pltpu.VMEM((depth, shape[1]), jnp.bfloat16), pltpu.VMEM((rows, depth), jnp.bfloat16)]
            + ([pltpu.VMEM(shape, jnp.bfloat16), pltpu.SemaphoreType.DMA((rows // 256 * (shape[1] // 256),))] if far else []),
            cost_estimate=pl.CostEstimate(
                flops=2 * depth * math.prod(shape), bytes_accessed=4 * math.prod(shape), transcendentals=0
            ),
            compiler_params=pltpu.CompilerParams(vmem_limit_bytes=32 * 2**20),
            name="image",
        )(tables, *[arrays[i] for i in used], *total)
        total = [image]
    return image.reshape(2, ANGLES, shape[1])


def partner(array, axis, apart):
    return lax.ppermute(array, axis, [(i, i ^ 1 << apart) for i in range(lax.axis_size(axis))])


def merge_levels(received, pulse_count, sub_pulses, depth_count):
    half = ANGLES // 2
    sub_index = lax.axis_index("sub")
    steering = to_bf16(by_source(real_form(steer_table(sub_pulses)), pulse_count))
    current = jnp.dot(steering, received, preferred_element_type=jnp.float32).astype(jnp.bfloat16)
    current = current.reshape(2, ANGLES, -1)
    sector = jnp.zeros((), jnp.int32)
    interp = jnp.asarray(interp_table(), jnp.float32)
    for depth in range(1, depth_count + 1):
        side_bit = sub_index // 2 ** (depth - 1) % 2
        sent = lax.dynamic_slice_in_dim(current, (1 - side_bit) * half, half, axis=1)
        kept = lax.dynamic_slice_in_dim(current, side_bit * half, half, axis=1)
        arrived = partner(sent, "sub", depth - 1)
        sector = 2 * sector + side_bit
        modulus = ANGLES * 2 ** (depth + 3)
        numerator = 2 * (sector * ANGLES + jnp.arange(ANGLES, dtype=jnp.int32)) + 1 - ANGLES * 2**depth
        center = (2 * side_bit - 1) * (sub_pulses * 2 ** (depth - 1) // 2)
        total = 0.0
        for child, place in ((kept, center), (arrived, -center)):
            turns = jnp.mod(place * numerator, modulus).astype(jnp.float32) / modulus
            cosine = (jnp.cos(TWO_PI * turns) * math.sqrt(0.5))[:, None] * interp
            sine_part = (-jnp.sin(TWO_PI * turns) * math.sqrt(0.5))[:, None] * interp
            table = jnp.stack([jnp.stack([cosine, -sine_part]), jnp.stack([sine_part, cosine])])
            total = total + jnp.einsum(
                "akjh,khg->ajg", table.astype(jnp.bfloat16), child, preferred_element_type=jnp.float32
            )
        current = total.astype(jnp.bfloat16)
    return current


def swap(array, even, odd=None):
    count = 2 * lax.axis_size("gate")
    pairs = [(i, i ^ (even if odd is None or i % 2 == 0 else odd)) for i in range(count)]
    return lax.ppermute(array, ("sub", "gate"), pairs)


CORE, Y, Z, FAR = 1, 2, 4, 8


def after(array, other):
    return lax.optimization_barrier((array, other))[0]


EXCHANGES = [((1, 0), (0, Y)), ((1, Y), (1, 0)), ((0, Y), (1, Y))]


def corner_turn(send):
    plan = [[place * Z, place * Z + Y] for place in range(4)]
    plan.append([place * Z + CORE + y for place in (0, 1, 3) for y in (0, Y)])
    plan.append([2 * Z + CORE, 2 * Z + CORE + Y])
    here, one, two, three, mates, mates_two = send(plan)
    width = here.shape[-1]
    mates = swap(mates, CORE)
    mates_two = swap(after(mates_two, mates), CORE)
    mates = mates.reshape(3, 2, -1, width)
    two = swap(two, 2 * Z)
    one = swap(jnp.stack([one, mates[1]], axis=1), Z)
    three = swap(jnp.stack([three, mates[2]], axis=1), 3 * Z)
    mates_two = swap(mates_two, 2 * Z)
    two = after(two, one)
    here = jnp.stack([here, mates[0]], axis=1)
    groups = [
        ([here[0], one[0], two[:1]], [here[1], one[1], two[1:]], [0, CORE, Z, Z + CORE, FAR]),
        ([mates_two[:1], three[0]], [mates_two[1:], three[1]], [FAR + CORE, FAR + Z, FAR + Z + CORE]),
    ]
    first_core = lax.axis_index("gate") % 2 == 0
    across = lax.axis_size("gate")
    arrays, places = [], []
    for home, away, apart in groups:
        home, away = jnp.concatenate(home), jnp.concatenate(away)
        arrays.append(home)
        places.append(((0, 0), (0, 0), apart))
        for even, odd in EXCHANGES:
            blocks = [away if along else home for _, along in (even, odd)]
            sent = away if even[1] and odd[1] else jnp.where(first_core, *blocks)
            arrays.append(swap(sent, *(side * across + along for side, along in (even, odd))))
            places.append((even, odd, apart))
    return arrays, places


def per_device(raw_echo, delays):
    gate_count = lax.axis_size("gate")
    sub_count = lax.axis_size("sub")
    pulse_count = raw_echo.shape[1]
    sub_pulses = pulse_count * gate_count
    depth_count = sub_count.bit_length() - 1
    send = functools.partial(range_compress, raw_echo, delays, depth_count, sub_pulses)
    if (sub_count, gate_count) != (2, 16):
        (compressed,) = send([range(gate_count)])
        me = lax.axis_index("gate")
        ordered = compressed[me ^ jnp.arange(gate_count)]
        received = lax.all_to_all(ordered, "gate", split_axis=0, concat_axis=0, tiled=True)
        received = received.reshape(2 * sub_pulses, SAMPLES // gate_count)
        return merge_levels(received, pulse_count, sub_pulses, depth_count)
    arrays, places = corner_turn(send)
    return form_image(image_tables(sub_pulses, pulse_count), arrays, places)


def solution(mesh):
    placed = (P(None, ("sub", "gate"), None), P(("sub", "gate")))
    return jax.shard_map(
        per_device, mesh=mesh, in_specs=placed, out_specs=P(None, "sub", "gate"), check_vma=False
    )
```

```python
import functools
import math

import jax
import jax.numpy as jnp
import numpy as np
from jax import lax
from jax.experimental import pallas as pl
from jax.experimental.pallas import tpu as pltpu
from jax.sharding import PartitionSpec as P

RADIX = 128
SAMPLES = 16384
ANGLES = 256
DELAY_MAX = 64
LANES = 128
RAW_PIECES = 4
ROWS = RADIX + DELAY_MAX


TWO_PI = 2.0 * math.pi


def to_bf16(values):
    return np.asarray(values, np.float32).astype(jnp.bfloat16)


def rounded(values):
    return to_bf16(values).astype(np.float64)


def real_form(table):
    upper = np.concatenate([table.real, -table.imag], axis=1)
    lower = np.concatenate([table.imag, table.real], axis=1)
    return np.concatenate([upper, lower], axis=0)


def unit(phases):
    return np.cos(phases) + 1j * np.sin(phases)


def dft_table():
    counter = np.arange(RADIX)
    table = unit(-TWO_PI / RADIX * (counter[:, None] * counter[None, :] % RADIX)) / math.sqrt(RADIX)
    return rounded(table.real) + 1j * rounded(table.imag)


def twiddles():
    phases = -TWO_PI / SAMPLES * (np.arange(ROWS)[:, None] * np.arange(RADIX)[None, :])
    return np.stack([np.cos(phases), np.sin(phases)]).astype(np.float32)


def near_phases(depth_count, sub_pulses):
    centers = [sub_pulses * 2 ** (depth - 1) // 2 for depth in range(1, depth_count + 1)]
    center_sq = float(sum(center * center for center in centers))
    phases = -TWO_PI / (4 * ANGLES) * center_sq / (16.0 * (SAMPLES + np.arange(SAMPLES)))
    return np.stack([np.cos(phases), np.sin(phases)]).astype(np.float32).reshape(2, RADIX, RADIX)


def steer_table(sub_pulses):
    modulus = 16 * ANGLES
    beams = 2 * np.arange(ANGLES) - ANGLES + 1
    pulses = 2 * np.arange(sub_pulses) - sub_pulses + 1
    table = unit(-TWO_PI / modulus * (beams[:, None] * pulses[None, :] % modulus)) / math.sqrt(sub_pulses)
    return rounded(table.real) + 1j * rounded(table.imag)


def interp_table():
    distance = np.arange(ANGLES)[:, None] * 0.5 - 0.25 - np.arange(ANGLES // 2)[None, :]
    taper = np.where(np.abs(distance) < 4.0, 0.5 + 0.5 * np.cos(math.pi * distance / 4.0), 0.0)
    return rounded(np.sinc(distance) * taper)


def merge_table(depth, sector, center):
    modulus = ANGLES * 2 ** (depth + 3)
    row_index = sector * ANGLES + np.arange(ANGLES)
    numerator = 2 * row_index + 1 - ANGLES * 2**depth
    turns = (center * numerator) % modulus / modulus
    return unit(-TWO_PI * turns)[:, None] * interp_table() / math.sqrt(2.0)


def by_source(table, pulse_count):
    rows = table.shape[0]
    return table.reshape(rows, 2, -1, pulse_count).transpose(0, 2, 1, 3).reshape(rows, -1)


def image_tables(sub_pulses, pulse_count):
    half = ANGLES // 2
    steer = steer_table(sub_pulses)
    tables = []
    for sub in range(2):
        beams = steer[sub * half : (sub + 1) * half]
        own = (2 * sub - 1) * (sub_pulses // 2)
        parts = [real_form(merge_table(1, sub, center) @ beams) for center in (own, -own)]
        tables.append(np.concatenate([by_source(part, pulse_count) for part in parts], axis=1))
    return to_bf16(np.stack(tables))


def compress_kernel(plan, delays_far, raw_far, dft_far, twiddle_far, near_far, *refs):
    outs, scratch = refs[: len(plan)], refs[len(plan) :]
    delays, raw, dft, twiddle, near, arrived, lines, grid_in, section, twisted, turned = scratch
    pulse_count = raw.shape[1]
    width = outs[0].shape[-1]
    me = lax.axis_index("gate")
    span = RADIX * pulse_count
    piece = SAMPLES // RAW_PIECES
    pieces = [
        pltpu.make_async_copy(
            raw_far.at[:, :, pl.ds(index * piece, piece)],
            raw.at[:, :, pl.ds(index * piece, piece)],
            arrived.at[index],
        )
        for index in range(RAW_PIECES)
    ]
    tables = [
        pltpu.make_async_copy(far, here, arrived.at[RAW_PIECES + index])
        for index, (far, here) in enumerate(
            ((dft_far, dft), (delays_far, delays), (twiddle_far, twiddle), (near_far, near))
        )
    ]
    for copy in pieces + tables:
        copy.start()
    for step in range(RADIX):
        if step * LANES % piece == 0:
            pieces[step * LANES // piece].wait()
        for part in range(2):
            lines[pl.ds(part * span + step * pulse_count, pulse_count), :] = raw[
                part, :, pl.ds(step * LANES, LANES)
            ].astype(jnp.float32)
    for part in range(2):
        for pulse in range(pulse_count):
            grid_in[pl.ds(part * RADIX, RADIX), pl.ds(pulse * LANES, LANES)] = lines[
                pl.ds(part * span + pulse, RADIX, stride=pulse_count), :
            ].astype(jnp.bfloat16)
    tables[0].wait()
    for first in range(0, pulse_count, 4):
        columns = pl.ds(first * LANES, 4 * LANES)
        sums = jnp.dot(dft[...], grid_in[:, columns], preferred_element_type=jnp.float32)
        for pulse in range(first, first + 4):
            for part in range(2):
                own = sums[
                    part * RADIX : (part + 1) * RADIX, (pulse - first) * LANES : (pulse - first + 1) * LANES
                ]
                section[pulse, part, pl.ds(0, RADIX), :] = own
                section[pulse, part, pl.ds(RADIX, DELAY_MAX), :] = own[:DELAY_MAX]
    tables[1].wait()
    tables[2].wait()
    for pulse in range(pulse_count):
        window = pl.ds(delays[pulse], RADIX)
        real_part = section[pulse, 0, window, :]
        imag_part = section[pulse, 1, window, :]
        cosine = twiddle[0, window, :]
        sine_part = twiddle[1, window, :]
        rows = pl.ds(pulse * RADIX, RADIX)
        twisted[rows, pl.ds(0, LANES)] = (real_part * cosine - imag_part * sine_part).astype(jnp.bfloat16)
        twisted[rows, pl.ds(LANES, LANES)] = (real_part * sine_part + imag_part * cosine).astype(jnp.bfloat16)
    tables[3].wait()
    last_rows = RADIX - 8
    gates = (
        lax.broadcasted_iota(jnp.int32, (8, LANES), 0) + last_rows
    ) * LANES + lax.broadcasted_iota(jnp.int32, (8, LANES), 1)
    cosine, sine_part = near[0], near[1]
    for first in range(0, pulse_count, 4):
        sums = lax.dot_general(
            dft[...],
            twisted[pl.ds(first * RADIX, 4 * RADIX), :],
            (((1,), (1,)), ((), ())),
            preferred_element_type=jnp.float32,
        )
        for pulse in range(first, first + 4):
            own = sums[:, (pulse - first) * LANES : (pulse - first + 1) * LANES]
            real_part, imag_part = own[:RADIX], own[RADIX:]
            parts = (
                real_part * cosine - imag_part * sine_part,
                real_part * sine_part + imag_part * cosine,
            )
            inside = gates < SAMPLES - delays[pulse]
            for part, values in enumerate(parts):
                start = part * span + pulse
                turned[pl.ds(start, last_rows, stride=pulse_count), :] = values[:last_rows]
                turned[pl.ds(start + last_rows * pulse_count, 8, stride=pulse_count), :] = jnp.where(
                    inside, values[last_rows:], 0.0
                )
    block_rows = width // LANES * pulse_count
    for out, places in zip(outs, plan, strict=True):
        for index, apart in enumerate(places):
            start = pl.multiple_of((me ^ apart) * block_rows, block_rows)
            for step in range(width // LANES):
                rows = pl.ds(start + step * pulse_count, pulse_count)
                imag_rows = pl.ds(span + start + step * pulse_count, pulse_count)
                both = jnp.concatenate([turned[rows, :], turned[imag_rows, :]], axis=0)
                out[index, :, pl.ds(step * LANES, LANES)] = both.astype(jnp.bfloat16)


def range_compress(raw_echo, delays, depth_count, sub_pulses, plan):
    gate_count = lax.axis_size("gate")
    pulse_count = raw_echo.shape[1]
    width = SAMPLES // gate_count
    span = RADIX * pulse_count
    dft = to_bf16(real_form(dft_table()))
    twiddle, near = twiddles(), near_phases(depth_count, sub_pulses)
    return pl.pallas_call(
        functools.partial(compress_kernel, plan),
        out_shape=[
            pltpu.VMEM((len(places), 2 * pulse_count, width), jnp.bfloat16) for places in plan
        ],
        in_specs=[pl.BlockSpec(memory_space=pltpu.HBM)] * 5,
        out_specs=[pl.BlockSpec(memory_space=pltpu.VMEM)] * len(plan),
        scratch_shapes=[
            pltpu.SMEM(delays.shape, delays.dtype),
            pltpu.VMEM(raw_echo.shape, raw_echo.dtype),
            pltpu.VMEM(dft.shape, dft.dtype),
            pltpu.VMEM(twiddle.shape, twiddle.dtype),
            pltpu.VMEM(near.shape, near.dtype),
            pltpu.SemaphoreType.DMA((RAW_PIECES + 4,)),
            pltpu.VMEM((2 * span + pulse_count, LANES), jnp.float32),
            pltpu.VMEM((2 * RADIX, pulse_count * LANES), jnp.bfloat16),
            pltpu.VMEM((pulse_count, 2, ROWS, LANES), jnp.float32),
            pltpu.VMEM((span, 2 * LANES), jnp.bfloat16),
            pltpu.VMEM((2 * span + pulse_count, LANES), jnp.float32),
        ],
        compiler_params=pltpu.CompilerParams(vmem_limit_bytes=60 * 2**20),
        name="compress",
    )(delays, raw_echo, dft, twiddle, near)


def image_kernel(plan, far, has_total, table, *refs):
    arrays, refs = refs[: len(plan)], refs[len(plan) :]
    if has_total:
        total, columns, out_far, data, out, sent = refs
    else:
        out, columns_next, data, columns = refs
    half = data.shape[0] // 2
    block = arrays[0].shape[1]
    me = lax.axis_index("gate")
    lower = (me ^ far) // FAR * half
    core = me % 2
    for array, ((side, along), (side_odd, along_odd), places) in zip(arrays, plan, strict=True):
        side = side + core * (side_odd - side)
        along = along + core * (along_odd - along)
        for index, apart in enumerate(places):
            if apart // FAR * FAR == far:
                start = side * half + (me ^ (apart + along)) * block - lower
                data[pl.ds(pl.multiple_of(start, block), block), :] = array[index]
    for side in range(0 if has_total else 2):
        for part, begin in ((columns, lower), (columns_next, half - lower)):
            source = pl.multiple_of(side * 2 * half + begin, half)
            part[:, pl.ds(side * half, half)] = table[lax.axis_index("sub"), :, pl.ds(source, half)]
    tile = 256
    copies = []
    for row in range(0, out.shape[0], tile):
        for column in range(0, out.shape[1], tile):
            place = pl.ds(row, tile), pl.ds(column, tile)
            sums = jnp.dot(columns[place[0], :], data[:, place[1]], preferred_element_type=jnp.float32)
            if has_total:
                sums = sums + total[place]
            out[place] = sums.astype(out.dtype)
            if has_total:
                copies.append(pltpu.make_async_copy(out.at[place], out_far.at[place], sent.at[len(copies)]))
                copies[-1].start()
    for copy in copies:
        copy.wait()


def form_image(tables, arrays, plan):
    rows, depth = tables.shape[1], tables.shape[2] // 2
    shape = rows, arrays[0].shape[-1]
    vmem = pl.BlockSpec(memory_space=pltpu.VMEM)
    total = []
    for far in (0, FAR):
        used = [i for i, (*_, places) in enumerate(plan) if any(apart // FAR * FAR == far for apart in places)]
        image = pl.pallas_call(
            functools.partial(image_kernel, [plan[i] for i in used], far, bool(total)),
            out_shape=jax.ShapeDtypeStruct(shape, jnp.bfloat16)
            if far
            else [pltpu.VMEM(shape, jnp.float32), pltpu.VMEM((rows, depth), jnp.bfloat16)],
            in_specs=[vmem] * (1 + len(used) + len(total)),
            out_specs=pl.BlockSpec(memory_space=pltpu.HBM) if far else [vmem, vmem],
            scratch_shapes=[pltpu.VMEM((depth, shape[1]), jnp.bfloat16)]
            + ([pltpu.VMEM(shape, jnp.bfloat16), pltpu.SemaphoreType.DMA((rows // 256 * (shape[1] // 256),))] if far else [pltpu.VMEM((rows, depth), jnp.bfloat16)]),
            cost_estimate=pl.CostEstimate(
                flops=2 * depth * math.prod(shape), bytes_accessed=4 * math.prod(shape), transcendentals=0
            ),
            compiler_params=pltpu.CompilerParams(vmem_limit_bytes=32 * 2**20),
            name="image",
        )(tables, *[arrays[i] for i in used], *total)
        total = image
    return image.reshape(2, ANGLES, shape[1])


def partner(array, axis, apart):
    return lax.ppermute(array, axis, [(i, i ^ 1 << apart) for i in range(lax.axis_size(axis))])


def merge_levels(received, pulse_count, sub_pulses, depth_count):
    half = ANGLES // 2
    sub_index = lax.axis_index("sub")
    steering = to_bf16(by_source(real_form(steer_table(sub_pulses)), pulse_count))
    current = jnp.dot(steering, received, preferred_element_type=jnp.float32).astype(jnp.bfloat16)
    current = current.reshape(2, ANGLES, -1)
    sector = jnp.zeros((), jnp.int32)
    interp = jnp.asarray(interp_table(), jnp.float32)
    for depth in range(1, depth_count + 1):
        side_bit = sub_index // 2 ** (depth - 1) % 2
        sent = lax.dynamic_slice_in_dim(current, (1 - side_bit) * half, half, axis=1)
        kept = lax.dynamic_slice_in_dim(current, side_bit * half, half, axis=1)
        arrived = partner(sent, "sub", depth - 1)
        sector = 2 * sector + side_bit
        modulus = ANGLES * 2 ** (depth + 3)
        numerator = 2 * (sector * ANGLES + jnp.arange(ANGLES, dtype=jnp.int32)) + 1 - ANGLES * 2**depth
        center = (2 * side_bit - 1) * (sub_pulses * 2 ** (depth - 1) // 2)
        total = 0.0
        for child, place in ((kept, center), (arrived, -center)):
            turns = jnp.mod(place * numerator, modulus).astype(jnp.float32) / modulus
            cosine = (jnp.cos(TWO_PI * turns) * math.sqrt(0.5))[:, None] * interp
            sine_part = (-jnp.sin(TWO_PI * turns) * math.sqrt(0.5))[:, None] * interp
            table = jnp.stack([jnp.stack([cosine, -sine_part]), jnp.stack([sine_part, cosine])])
            total = total + jnp.einsum(
                "akjh,khg->ajg", table.astype(jnp.bfloat16), child, preferred_element_type=jnp.float32
            )
        current = total.astype(jnp.bfloat16)
    return current


def swap(array, even, odd=None):
    count = 2 * lax.axis_size("gate")
    pairs = [(i, i ^ (even if odd is None or i % 2 == 0 else odd)) for i in range(count)]
    return lax.ppermute(array, ("sub", "gate"), pairs)


CORE, Y, Z, FAR = 1, 2, 4, 8


def after(array, other):
    return lax.optimization_barrier((array, other))[0]


EXCHANGES = [((1, 0), (0, Y)), ((1, Y), (1, 0)), ((0, Y), (1, Y))]


def corner_turn(send):
    plan = [[place * Z, place * Z + Y] for place in range(4)]
    plan.append([place * Z + CORE + y for place in (0, 1, 3) for y in (0, Y)])
    plan.append([2 * Z + CORE, 2 * Z + CORE + Y])
    here, one, two, three, mates, mates_two = send(plan)
    width = here.shape[-1]
    mates = swap(mates, CORE)
    mates_two = swap(after(mates_two, mates), CORE)
    mates = mates.reshape(3, 2, -1, width)
    two = swap(two, 2 * Z)
    one = swap(jnp.stack([one, mates[1]], axis=1), Z)
    three = swap(jnp.stack([three, mates[2]], axis=1), 3 * Z)
    mates_two = swap(mates_two, 2 * Z)
    two = after(two, one)
    here = jnp.stack([here, mates[0]], axis=1)
    groups = [
        ([here[0], one[0], two[:1]], [here[1], one[1], two[1:]], [0, CORE, Z, Z + CORE, FAR]),
        ([mates_two[:1], three[0]], [mates_two[1:], three[1]], [FAR + CORE, FAR + Z, FAR + Z + CORE]),
    ]
    first_core = lax.axis_index("gate") % 2 == 0
    across = lax.axis_size("gate")
    arrays, places = [], []
    for home, away, apart in groups:
        home, away = jnp.concatenate(home), jnp.concatenate(away)
        arrays.append(home)
        places.append(((0, 0), (0, 0), apart))
        for even, odd in EXCHANGES:
            blocks = [away if along else home for _, along in (even, odd)]
            sent = away if even[1] and odd[1] else jnp.where(first_core, *blocks)
            arrays.append(swap(sent, *(side * across + along for side, along in (even, odd))))
            places.append((even, odd, apart))
    return arrays, places


def per_device(raw_echo, delays):
    gate_count = lax.axis_size("gate")
    sub_count = lax.axis_size("sub")
    pulse_count = raw_echo.shape[1]
    sub_pulses = pulse_count * gate_count
    depth_count = sub_count.bit_length() - 1
    send = functools.partial(range_compress, raw_echo, delays, depth_count, sub_pulses)
    if (sub_count, gate_count) != (2, 16):
        (compressed,) = send([range(gate_count)])
        me = lax.axis_index("gate")
        ordered = compressed[me ^ jnp.arange(gate_count)]
        received = lax.all_to_all(ordered, "gate", split_axis=0, concat_axis=0, tiled=True)
        received = received.reshape(2 * sub_pulses, SAMPLES // gate_count)
        return merge_levels(received, pulse_count, sub_pulses, depth_count)
    arrays, places = corner_turn(send)
    return form_image(image_tables(sub_pulses, pulse_count), arrays, places)


def solution(mesh):
    placed = (P(None, ("sub", "gate"), None), P(("sub", "gate")))
    return jax.shard_map(
        per_device, mesh=mesh, in_specs=placed, out_specs=P(None, "sub", "gate"), check_vma=False
    )
```
